32 devices in a mesh: dp: 4 (over y, x), vocab: 8 (over z, core).
Axes of the slice: x: 2, y: 2, z: 4, core: 2. Of those that a mesh axis runs over, the one named last changes fastest.
Arguments:
- hidden_states: bfloat16 [512, 4096], P('dp', 'vocab'), may hold values from -6 to 6
- teacher_logprob: bfloat16 [512, 8192], P(('dp', 'vocab')), may hold values from -12 to -0.5
- head_weight: bfloat16 [4096, 8192], P('dp', 'vocab'), may hold values from -6 to 6
- token_ids: int32 [512], P('dp'), may hold values from 0 to 8191
- padding_mask: int32 [512], P('dp'), may hold values 0 or 1
Outputs:
- logit_grad: bfloat16 [512, 8192], P('dp', 'vocab')
- hidden_grad: float32 [512, 4096], P('dp', 'vocab')
- head_grad: bfloat16 [4096, 8192], P('dp', 'vocab')
The draws below stay inside these ranges and needn't reach their ends.
All inputs are finite; a program needn't handle non-finite values. No bound on the sum of `padding_mask` on one device may be relied on, other than what follows from the above.
Results may differ from the reference program's by a relative error of at most 0.012.
Values may be sent and summed in bfloat16 or wider, within the bound.
A program may use at most 64 MiB of HBM per device.

```python
import math
import jax
import jax.numpy as jnp
import numpy as np
from jax import lax

D = 4096
TOK_DEV = 128
TOKENS = 512
V = 8192


def hidden_rows(key, row_spread):
    key_normal = jax.random.fold_in(jax.random.fold_in(key, 11), 0)
    key_scale = jax.random.fold_in(jax.random.fold_in(key, 11), 2)
    normal_part = jnp.clip(jax.random.normal(key_normal, (TOKENS, D), jnp.float32), -6.0, 6.0)
    base = normal_part
    scales = jnp.exp(row_spread * jax.random.uniform(key_scale, (TOKENS, 1), jnp.float32, -1.0, 1.0))
    return (base, scales)


def draw_hidden_states(key, part):
    rows, scales = hidden_rows(key, 0.0)
    return rows.astype(jnp.bfloat16)


def draw_head_weight(key, part):
    rows, scales = hidden_rows(key, 0.0)
    strength = 0.0
    key = jax.random.fold_in(key, 5)
    key_entries, key_scale, key_pick, key_first, key_second, key_gap = jax.random.split(key, 6)
    ramp = jnp.exp(0.2623643 * jnp.arange(V, dtype=jnp.float32) / V)
    column_scale = jnp.exp(jax.random.uniform(key_scale, (1, V), jnp.float32, -0.2876821, 2.014903)) * ramp[None, :]
    entries = jnp.clip(jax.random.normal(key_entries, (D, V), jnp.float32), -6.0, 6.0) * column_scale / D ** 0.5
    picked = jax.random.randint(key_pick, (6,), 0, TOKENS)
    first_cols = jax.random.randint(key_first, (6,), 0, V)
    second_cols = jax.random.randint(key_second, (6,), 0, V)
    levels = jnp.array([110.0, 160.0, 230.0, 300.0, 140.0, 260.0], jnp.float32)
    gaps = jax.random.uniform(key_gap, (6,), jnp.float32, 1.0, 3.0)
    aligned = rows[picked] / (D * scales[picked] ** 2)
    entries = entries.at[:, first_cols].add(strength * (aligned * levels[:, None]).T)
    entries = entries.at[:, second_cols].add(strength * (aligned * (levels - gaps)[:, None]).T)
    return entries.astype(jnp.bfloat16)


def place_ends(values, key, low, top_value):
    extent = values.shape
    place = [jax.random.randint(jax.random.fold_in(key, axis), (), 0, extent[axis]) for axis in range(len(extent))]
    values = values.at[tuple(place)].set(low)
    longest = extent.index(max(extent))
    place[longest] = (place[longest] + 1) % extent[longest]
    return values.at[tuple(place)].set(top_value)


def block_levels(stream_key, dims, pieces, low, top_value):
    loudness, own = 1.0, jax.random.fold_in(stream_key, 6)
    for position, blocks in pieces:
        heights = jnp.exp(jax.random.uniform(jax.random.fold_in(own, position), (blocks,), jnp.float32, low / len(pieces), top_value / len(pieces)))
        loudness = loudness * jnp.repeat(heights, dims[position] // blocks).reshape([-1 if axis == position else 1 for axis in range(len(dims))])
    return loudness


def rank_table(count, skew):
    portions = [(1 << 20) // math.isqrt(rank ** skew) + 1 for rank in range(1, count + 1)]
    scale = 1 + sum(portions) // (1 << 30)
    return np.cumsum(np.array([max(1, weight // scale) for weight in portions]))


def ranked_ids(key, dims, count, lean):
    grid = rank_table(count, lean)
    pick = jax.random.randint(jax.random.fold_in(key, 1), dims, 0, int(grid[count - 1]))
    rank = jnp.searchsorted(jnp.asarray(grid, jnp.int32), pick, side="right")
    return jax.random.permutation(jax.random.fold_in(key, 2), count)[rank].astype(jnp.int32)


def setup_inputs(seed: int = 0) -> dict:
    key_of = jax.random.split(jax.random.key(seed), 6)
    hidden_states = draw_hidden_states(jax.random.fold_in(key_of[5], 71), 0)
    teacher_logprob = jnp.clip(-12.0 + 11.5 * jax.random.uniform(key_of[1], (TOKENS, V), jnp.float32) ** block_levels(key_of[1], (TOKENS, V), ((0, 32),), -0.2, 0.2), -12.0, -0.5).astype(jnp.bfloat16)
    head_weight = draw_head_weight(jax.random.fold_in(key_of[5], 71), 0)
    token_ids = place_ends(ranked_ids(key_of[3], (TOKENS,), V, 2), jax.random.fold_in(key_of[3], 3), 0, V - 1).astype(jnp.int32)
    padding_mask = place_ends((jax.random.randint(key_of[4], (TOKENS,), 0, 8) < 7).astype(jnp.int32), jax.random.fold_in(key_of[4], 1), 0, 1)
    return dict(hidden_states=hidden_states, teacher_logprob=teacher_logprob, head_weight=head_weight, token_ids=token_ids, padding_mask=padding_mask)


anchor_weight = 0.25


def reference(hidden_states, teacher_logprob, head_weight, token_ids, padding_mask):
    rows_total = hidden_states.shape[0]
    width = hidden_states.shape[1]
    vocab = head_weight.shape[1]
    blocks = rows_total // TOK_DEV
    columns = jnp.arange(vocab, dtype=jnp.int32)

    def one_block(carry, index):
        start = (index * TOK_DEV).astype(jnp.int32)
        hidden = lax.dynamic_slice_in_dim(hidden_states, start, TOK_DEV, 0)
        teacher = lax.dynamic_slice_in_dim(teacher_logprob, start, TOK_DEV, 0).astype(jnp.float32)
        ids = lax.dynamic_slice_in_dim(token_ids, start, TOK_DEV, 0)
        keep = lax.dynamic_slice_in_dim(padding_mask, start, TOK_DEV, 0).astype(jnp.float32)
        logits = jnp.dot(hidden, head_weight, preferred_element_type=jnp.float32)
        top = jnp.max(logits, axis=1, keepdims=True)
        expo = jnp.exp(logits - top)
        total = jnp.sum(expo, axis=1, keepdims=True)
        gap = logits - teacher
        weighted = jnp.sum(expo * gap, axis=1, keepdims=True)
        prob = expo / total
        onehot = (columns[None, :] == ids[:, None]).astype(jnp.float32)
        grad = keep[:, None] * (prob * (gap - weighted / total) + anchor_weight * (prob - onehot))
        grad = grad.astype(jnp.bfloat16)
        back = lax.dot_general(grad, head_weight, (((1,), (1,)), ((), ())), preferred_element_type=jnp.float32)
        return carry, (grad, back)

    unused, outputs = lax.scan(one_block, jnp.zeros((), jnp.float32), jnp.arange(blocks, dtype=jnp.int32))
    logit_grad = outputs[0].reshape(rows_total, vocab)
    hidden_grad = outputs[1].reshape(rows_total, width)
    block_width = width // 8

    def weight_rows(index):
        start = (index * block_width).astype(jnp.int32)
        piece = lax.dynamic_slice_in_dim(hidden_states, start, block_width, 1)
        product = lax.dot_general(piece, logit_grad, (((0,), (0,)), ((), ())), preferred_element_type=jnp.float32)
        return product.astype(jnp.bfloat16)

    head_grad = lax.map(weight_rows, jnp.arange(8, dtype=jnp.int32)).reshape(width, vocab)
    return logit_grad, hidden_grad, head_grad
```

```python
import functools
import jax
import jax.numpy as jnp
from jax import lax
from jax.experimental import pallas as pl
from jax.experimental.pallas import tpu as pltpu
from jax.sharding import PartitionSpec as P

anchor_weight = 0.25
MESH = pl.DeviceIdType.MESH
F32 = jnp.float32
BF16 = jnp.bfloat16


def kernel(
    hid_ref, tea_ref, head_ref, ids_ref, mask_ref,
    lg_out, hg_out, wg_out,
    head_v, zbuf, hblk, hid_t, tea_v, part, relay, got, logits_v, stat_v, lgb,
    hown, sib_out, sib_in, d1_out, d1_in, d2_in, wg_v, hg_v,
    loc_sem, a1s, a1r, a2s, a2r, a3s, a3r, ts, tr, bs, br, ss, sr, cs, cr,
    es, er, d1s, d1r, d2s, d2r, wsem,
):
    tok, feat = hid_ref.shape
    width, voc = head_ref.shape
    half = tok // 2
    trow = tea_ref.shape[0]
    i, j = lax.axis_index("dp"), lax.axis_index("vocab")
    z, c = j // 2, j % 2
    sib = z * 2 + (1 - c)
    nx = i + 1 - 2 * (i % 2)
    ny = (i + 2) % 4
    nd = 3 - i
    rel = (i, nx, ny, nd)

    def remote(src, dst, ssem, rsem, to):
        return pltpu.make_async_remote_copy(
            src_ref=src, dst_ref=dst, send_sem=ssem, recv_sem=rsem,
            device_id=to, device_id_type=MESH,
        )

    def rows(block, start=0, size=None):
        size = tok if size is None else size
        return pl.ds(pl.multiple_of(block * tok + start, 16), size)

    mine = pl.ds(pl.multiple_of(c * feat, feat), feat)
    other = pl.ds(pl.multiple_of((1 - c) * feat, feat), feat)

    cp_hid = pltpu.make_async_copy(hid_ref, zbuf.at[z], loc_sem.at[0])
    cp_head = pltpu.make_async_copy(head_ref, head_v, loc_sem.at[1])
    own_cols = pl.ds(pl.multiple_of(j * voc, voc), voc)
    own_trow = pl.ds(pl.multiple_of(j * trow, trow), trow)
    cp_tea = pltpu.make_async_copy(tea_ref.at[:, own_cols], tea_v.at[own_trow, :], loc_sem.at[2])
    cp_hid.start()
    cp_head.start()
    cp_tea.start()

    barrier = pltpu.get_barrier_semaphore()
    for k in range(1, 4):
        pl.semaphore_signal(barrier, inc=1, device_id={"dp": (i + k) % 4}, device_id_type=MESH)
    for k in range(1, 8):
        pl.semaphore_signal(barrier, inc=1, device_id={"vocab": (j + k) % 8}, device_id_type=MESH)
    pl.semaphore_wait(barrier, 10)

    a1 = []
    for k in range(1, 4):
        cp = remote(hid_ref, zbuf.at[z], a1s.at[k], a1r.at[k], {"vocab": ((z + k) % 4) * 2 + c})
        cp.start()
        a1.append(cp)
    cp_hid.wait()

    def a2_copy(zs, shift):
        return remote(
            zbuf.at[zs], hblk.at[rows(i), mine], a2s.at[shift], a2r.at[shift], {"dp": zs}
        )

    def a2_local(zs):
        return pltpu.make_async_copy(zbuf.at[zs], hblk.at[rows(i), mine], loc_sem.at[3])

    def forward(zs):
        shift = (zs - i + 4) % 4

        @pl.when(shift != 0)
        def _():
            a2_copy(zs, shift).start()

        @pl.when(shift == 0)
        def _():
            a2_local(zs).start()

    forward(z)
    for k in range(1, 4):
        a1[k - 1].wait_recv()
        forward((z - k + 4) % 4)

    tcps = []
    for k in range(1, 8):
        jt = (j + k) % 8
        cp = remote(
            tea_ref.at[:, pl.ds(pl.multiple_of(jt * voc, voc), voc)], tea_v.at[own_trow, :],
            ts.at[k], tr.at[k], {"vocab": jt},
        )
        cp.start()
        tcps.append(cp)

    a3 = []
    for k in range(4):
        src = (i - k + 4) % 4
        if k == 0:
            a2_local(i).wait()
        else:
            a2_copy((i + k) % 4, k).wait_recv()
        piece = hblk.at[rows(src), mine]
        cp = remote(piece, piece, a3s.at[k], a3r.at[k], {"vocab": sib})
        cp.start()
        a3.append(cp)
    cp_head.wait()
    for cp in a3:
        cp.wait_recv()

    def partial_logits(r):
        x = hblk[rows(rel[r]), :]

        @pl.loop(0, voc // 256)
        def _(t):
            col = pl.ds(pl.multiple_of(t * 256, 256), 256)
            part[r, :, col] = jnp.dot(x, head_v[:, col], preferred_element_type=F32)

    lo, hi = pl.ds(0, half), pl.ds(half, half)
    to_x, to_y, to_d = {"dp": nx}, {"dp": ny}, {"dp": nd}
    b = []

    def send_b(src, dst, to):
        n = len(b)
        cp = remote(src, dst, bs.at[n], br.at[n], to)
        cp.start()
        b.append(cp)

    partial_logits(3)
    send_b(part.at[3, lo, :], relay.at[0], to_x)
    send_b(part.at[3, hi, :], relay.at[1], to_y)
    partial_logits(1)
    send_b(part.at[1, lo, :], got.at[0, lo, :], to_x)
    partial_logits(2)
    send_b(part.at[2, hi, :], got.at[1, hi, :], to_y)
    partial_logits(0)

    @pl.loop(0, width // 256)
    def _(t):
        cut = pl.ds(pl.multiple_of(t * 256, 256), 256)
        hid_t[cut, :] = jnp.swapaxes(hblk[:, cut], 0, 1)

    b[0].wait_recv()
    part[2, lo, :] = part[2, lo, :] + relay[0]
    send_b(part.at[2, lo, :], got.at[1, lo, :], to_y)
    b[1].wait_recv()
    part[1, hi, :] = part[1, hi, :] + relay[1]
    send_b(part.at[1, hi, :], got.at[0, hi, :], to_x)

    cp_tea.wait()
    for cp in tcps:
        cp.wait_recv()
    for n in (2, 3, 4, 5):
        b[n].wait_recv()

    logits = part[0] + got[0] + got[1]
    logits_v[...] = logits
    m = jnp.max(logits, axis=1, keepdims=True)
    e = jnp.exp(logits - m)
    s = jnp.sum(e, axis=1, keepdims=True)
    w = jnp.sum(e * (logits - tea_v[...].astype(F32)), axis=1, keepdims=True)
    lane = lax.broadcasted_iota(jnp.int32, (tok, tok), 1)
    packed = jnp.where(lane == 0, m, jnp.where(lane == 1, s, w))
    stat_v[j] = jnp.swapaxes(packed, 0, 1)[0:8, :]
    scps = []
    for k in range(1, 8):
        cp = remote(stat_v.at[j], stat_v.at[j], ss.at[k], sr.at[k], {"vocab": (j + k) % 8})
        cp.start()
        scps.append(cp)
    for cp in scps:
        cp.wait_recv()
    stats = stat_v[...]
    tops = stats[:, 0, :]
    top = jnp.max(tops, axis=0, keepdims=True)
    scale = jnp.exp(tops - top)
    total = jnp.sum(stats[:, 1, :] * scale, axis=0, keepdims=True)
    weighted = jnp.sum(stats[:, 2, :] * scale, axis=0, keepdims=True)
    sub = lax.broadcasted_iota(jnp.int32, (tok, tok), 0)
    table = jnp.where(sub == 0, top, jnp.where(sub == 1, total, jnp.where(
        sub == 2, weighted / total, jnp.where(
            sub == 3, ids_ref[...].astype(F32), mask_ref[...].astype(F32)))))
    table = jnp.swapaxes(table, 0, 1)
    logits = logits_v[...]
    prob = jnp.exp(logits - table[:, 0:1]) / table[:, 1:2]
    gap = logits - tea_v[...].astype(F32)
    ids = table[:, 3:4].astype(jnp.int32) - j * voc
    onehot = (lax.broadcasted_iota(jnp.int32, (tok, voc), 1) == ids).astype(F32)
    lg = table[:, 4:5] * (prob * (gap - table[:, 2:3]) + anchor_weight * (prob - onehot))
    lgb[rows(i), :] = lg.astype(BF16)

    cc = []

    def send_c(block, start, to):
        n = len(cc)
        piece = lgb.at[rows(block, start, half), :]
        cp = remote(piece, piece, cs.at[n], cr.at[n], to)
        cp.start()
        cc.append(cp)

    send_c(i, 0, to_x)
    send_c(i, half, to_y)
    send_c(i, half, to_x)
    send_c(i, 0, to_y)
    cp_lg = pltpu.make_async_copy(lgb.at[rows(i), :], lg_out, wsem.at[4])
    cp_lg.start()

    nt = (((1,), (1,)), ((), ()))
    ecps = []

    def hidden_part(r):
        g = lgb[rows(rel[r]), :]
        sib_out[r] = lax.dot_general(
            g, head_v[other, :], nt, preferred_element_type=F32).astype(BF16)
        cp = remote(sib_out.at[r], sib_in.at[r], es.at[r], er.at[r], {"vocab": sib})
        cp.start()
        ecps.append(cp)
        hown[r] = lax.dot_general(g, head_v[mine, :], nt, preferred_element_type=F32)

    hidden_part(0)
    cc[0].wait_recv()
    send_c(nx, 0, to_y)
    cc[1].wait_recv()
    send_c(ny, half, to_x)

    d1 = [None]

    def d2_copy(r, shift, zt):
        src = d1_in.at[r]
        return remote(src, d2_in.at[shift], d2s.at[shift], d2r.at[shift], {"vocab": zt * 2 + c})

    def d2_send(r):
        zt = rel[r]
        shift = (zt - z + 4) % 4

        @pl.when(shift != 0)
        def _():
            d2_copy(r, shift, zt).start()

        @pl.when(shift == 0)
        def _():
            d2_in[0] = d1_in[r]

    def reduced(r):
        ecps[r].wait_recv()
        summed = (hown[r] + sib_in[r].astype(F32)).astype(BF16)
        if r == 0:
            d1_in[0] = summed
            d2_send(0)
        else:
            d1_out[r] = summed
            cp = remote(d1_out.at[r], d1_in.at[r], d1s.at[r], d1r.at[r], (None, to_x, to_y, to_d)[r])
            cp.start()
            d1.append(cp)

    reduced(0)
    cc[2].wait_recv()
    hidden_part(1)
    cc[3].wait_recv()
    hidden_part(2)
    reduced(1)
    reduced(2)
    cc[4].wait_recv()
    cc[5].wait_recv()
    hidden_part(3)
    d1[1].wait_recv()
    d2_send(1)
    d1[2].wait_recv()
    d2_send(2)
    reduced(3)

    wcps = []
    quarter = width // 4

    def weight_part(t):
        cut = pl.ds(t * quarter, quarter)

        @pl.loop(0, voc // 256)
        def _(u):
            col = pl.ds(pl.multiple_of(u * 256, 256), 256)
            wg_v[cut, col] = jnp.dot(
                hid_t[cut, :], lgb[:, col], preferred_element_type=F32).astype(BF16)

        cp = pltpu.make_async_copy(wg_v.at[cut, :], wg_out.at[cut, :], wsem.at[t])
        cp.start()
        wcps.append(cp)

    weight_part(0)
    weight_part(1)
    d1[3].wait_recv()
    d2_send(3)
    weight_part(2)
    weight_part(3)

    for k in range(1, 4):
        d2_copy(0, k, (z + k) % 4).wait_recv()
    acc = d2_in[0].astype(F32)
    for k in range(1, 4):
        acc = acc + d2_in[k].astype(F32)
    hg_v[...] = acc
    cp_hg = pltpu.make_async_copy(hg_v, hg_out, wsem.at[5])
    cp_hg.start()

    for cp in a1 + tcps + a3 + b + scps + cc + ecps + d1[1:]:
        cp.wait_send()
    for k in range(1, 4):
        a2_copy((i + k) % 4, k).wait_send()
        d2_copy(0, k, (z + k) % 4).wait_send()
    for cp in wcps:
        cp.wait()
    cp_lg.wait()
    cp_hg.wait()


def fused(hidden_states, teacher_logprob, head_weight, token_ids, padding_mask):
    tok, feat = hidden_states.shape
    width, voc = head_weight.shape
    trow = teacher_logprob.shape[0]
    half = tok // 2
    any_spec = pl.BlockSpec(memory_space=pl.ANY)
    vmem_spec = pl.BlockSpec(memory_space=pltpu.VMEM)
    dma = pltpu.SemaphoreType.DMA
    return pl.pallas_call(
        kernel,
        out_shape=(
            jax.ShapeDtypeStruct((tok, voc), BF16),
            jax.ShapeDtypeStruct((tok, feat), F32),
            jax.ShapeDtypeStruct((width, voc), BF16),
        ),
        in_specs=[any_spec, any_spec, any_spec, vmem_spec, vmem_spec],
        out_specs=[any_spec] * 3,
        scratch_shapes=[
            pltpu.VMEM((width, voc), BF16),
            pltpu.VMEM((4, tok, feat), BF16),
            pltpu.VMEM((4 * tok, width), BF16),
            pltpu.VMEM((width, 4 * tok), BF16),
            pltpu.VMEM((8 * trow, voc), BF16),
            pltpu.VMEM((4, tok, voc), F32),
            pltpu.VMEM((2, half, voc), F32),
            pltpu.VMEM((2, tok, voc), F32),
            pltpu.VMEM((tok, voc), F32),
            pltpu.VMEM((8, 8, tok), F32),
            pltpu.VMEM((4 * tok, voc), BF16),
            pltpu.VMEM((4, tok, feat), F32),
            pltpu.VMEM((4, tok, feat), BF16),
            pltpu.VMEM((4, tok, feat), BF16),
            pltpu.VMEM((4, tok, feat), BF16),
            pltpu.VMEM((4, tok, feat), BF16),
            pltpu.VMEM((4, tok, feat), BF16),
            pltpu.VMEM((width, voc), BF16),
            pltpu.VMEM((tok, feat), F32),
            dma((4,)), dma((4,)), dma((4,)), dma((4,)), dma((4,)), dma((4,)), dma((4,)),
            dma((8,)), dma((8,)), dma((6,)), dma((6,)), dma((8,)), dma((8,)),
            dma((6,)), dma((6,)), dma((4,)), dma((4,)), dma((4,)), dma((4,)),
            dma((4,)), dma((4,)), dma((6,)),
        ],
        compiler_params=pltpu.CompilerParams(
            collective_id=0, has_side_effects=True, vmem_limit_bytes=40 * 1024 * 1024
        ),
        cost_estimate=pl.CostEstimate(
            flops=6 * 4 * tok * width * voc, bytes_accessed=6 * width * voc,
            transcendentals=2 * tok * voc,
        ),
    )(
        hidden_states, teacher_logprob, head_weight,
        token_ids.reshape(1, tok), padding_mask.reshape(1, tok),
    )


def gathered(n_dp, n_vocab, hidden_states, teacher_logprob, head_weight, token_ids, padding_mask):
    voc = head_weight.shape[1]
    full = lax.all_gather(hidden_states, "vocab", axis=1, tiled=True)
    block = lax.all_to_all(full, "dp", split_axis=1, concat_axis=0, tiled=True)
    teacher = lax.all_to_all(teacher_logprob, "vocab", split_axis=1, concat_axis=0, tiled=True)
    part = jnp.dot(block, head_weight, preferred_element_type=F32)
    logits = lax.psum_scatter(part, "dp", scatter_dimension=0, tiled=True)
    gap = logits - teacher.astype(F32)
    top = lax.pmax(jnp.max(logits, axis=1), "vocab")
    expo = jnp.exp(logits - top[:, None])
    total, weighted = lax.psum((jnp.sum(expo, axis=1), jnp.sum(expo * gap, axis=1)), "vocab")
    columns = lax.axis_index("vocab") * voc + jnp.arange(voc, dtype=jnp.int32)
    onehot = (columns[None, :] == token_ids[:, None]).astype(F32)
    prob = expo / total[:, None]
    keep = padding_mask.astype(F32)[:, None]
    logit_grad = (
        keep * (prob * (gap - (weighted / total)[:, None]) + anchor_weight * (prob - onehot))
    ).astype(BF16)
    every = lax.all_gather(logit_grad, "dp", axis=0, tiled=True)
    head_grad = lax.dot_general(
        block, every, (((0,), (0,)), ((), ())), preferred_element_type=F32).astype(BF16)
    back = lax.dot_general(
        every, head_weight, (((1,), (1,)), ((), ())), preferred_element_type=F32)
    back = lax.all_to_all(back, "dp", split_axis=0, concat_axis=1, tiled=True)
    hidden_grad = lax.psum_scatter(back, "vocab", scatter_dimension=1, tiled=True)
    return (logit_grad, hidden_grad, head_grad)


def solution(mesh):
    in_specs = (P("dp", "vocab"), P(("dp", "vocab"), None), P("dp", "vocab"), P("dp"), P("dp"))
    out_specs = (P("dp", "vocab"), P("dp", "vocab"), P("dp", "vocab"))
    n_dp, n_vocab = mesh.shape["dp"], mesh.shape["vocab"]
    body = fused if (n_dp, n_vocab) == (4, 8) else functools.partial(gathered, n_dp, n_vocab)
    return jax.shard_map(body, mesh=mesh, in_specs=in_specs, out_specs=out_specs, check_vma=False)
```

```python
import functools
import jax
import jax.numpy as jnp
from jax import lax
from jax.experimental import pallas as pl
from jax.experimental.pallas import tpu as pltpu
from jax.sharding import PartitionSpec as P

anchor_weight = 0.25
MESH = pl.DeviceIdType.MESH
F32 = jnp.float32
BF16 = jnp.bfloat16


def kernel(
    hid_ref, tea_ref, head_ref, ids_ref, mask_ref,
    lg_out, hg_out, wg_out,
    head_v, head_t, zbuf, hblk, hid_t, tea_v, ids_v, mask_v, part, relay, got, logits_v, stat_v,
    lgb, hown, sib_out, sib_in, d1_out, d1_in, d2_in, wg_v, hg_v,
    loc_sem, a1s, a1r, a2s, a2r, a3s, a3r, ts, tr, bs, br, ss, sr, cs, cr,
    es, er, d1s, d1r, d2s, d2r, wsem,
):
    tok, feat = hid_ref.shape
    width, voc = head_ref.shape
    half = tok // 2
    quart = half // 2
    group = 4 * half
    trow = tea_ref.shape[0]
    i, j = lax.axis_index("dp"), lax.axis_index("vocab")
    z, c = j // 2, j % 2
    sib = z * 2 + (1 - c)
    nx = i + 1 - 2 * (i % 2)
    ny = (i + 2) % 4
    nd = 3 - i
    rel = (i, nx, ny, nd)
    to_x, to_y, to_d = {"dp": nx}, {"dp": ny}, {"dp": nd}
    to_rel = (None, to_x, to_y, to_d)
    to_sib = {"vocab": sib}

    def remote(src, dst, ssem, rsem, to):
        return pltpu.make_async_remote_copy(
            src_ref=src, dst_ref=dst, send_sem=ssem, recv_sem=rsem,
            device_id=to, device_id_type=MESH,
        )

    def cut(block, begin=0, size=None):
        size = half if size is None else size
        return pl.ds(pl.multiple_of(block * half + begin, 16), size)

    def rows(h, block, begin=0, size=None):
        return cut(h * 4 + block, begin, size)

    mine = pl.ds(pl.multiple_of(c * feat, feat), feat)
    other = pl.ds(pl.multiple_of((1 - c) * feat, feat), feat)

    own_cols = pl.ds(pl.multiple_of(j * voc, voc), voc)
    own_trow = pl.ds(pl.multiple_of(j * trow, trow), trow)
    cp_hid = pltpu.make_async_copy(hid_ref, zbuf.at[z], loc_sem.at[0])
    cp_head = pltpu.make_async_copy(head_ref, head_v, loc_sem.at[1])
    cp_tea = pltpu.make_async_copy(tea_ref.at[:, own_cols], tea_v.at[own_trow, :], loc_sem.at[2])
    cp_ids = pltpu.make_async_copy(ids_ref, ids_v, loc_sem.at[3])
    cp_mask = pltpu.make_async_copy(mask_ref, mask_v, loc_sem.at[4])
    for cp in (cp_hid, cp_head, cp_tea, cp_ids, cp_mask):
        cp.start()

    barrier = pltpu.get_barrier_semaphore()
    for k in range(1, 4):
        pl.semaphore_signal(barrier, inc=1, device_id={"dp": (i + k) % 4}, device_id_type=MESH)
    for k in range(1, 8):
        pl.semaphore_signal(barrier, inc=1, device_id={"vocab": (j + k) % 8}, device_id_type=MESH)
    pl.semaphore_wait(barrier, 10)

    a1 = ([], [])

    def send_a1(h):
        piece = pl.ds(h * half, half)
        for k in range(1, 4):
            cp = remote(
                hid_ref.at[piece, :], zbuf.at[z, piece, :], a1s.at[h, k], a1r.at[h, k],
                {"vocab": ((z + k) % 4) * 2 + c},
            )
            cp.start()
            a1[h].append(cp)

    def a2_copy(h, zs, shift):
        return remote(
            zbuf.at[zs, pl.ds(h * half, half), :], hblk.at[rows(h, i), mine],
            a2s.at[h, shift], a2r.at[h, shift], {"dp": zs},
        )

    def a2_local(h, zs):
        return pltpu.make_async_copy(
            zbuf.at[zs, pl.ds(h * half, half), :], hblk.at[rows(h, i), mine], loc_sem.at[5 + h]
        )

    def forward(h, zs):
        shift = (zs - i + 4) % 4

        @pl.when(shift != 0)
        def _():
            a2_copy(h, zs, shift).start()

        @pl.when(shift == 0)
        def _():
            a2_local(h, zs).start()

    def forward_all(h):
        forward(h, z)
        for k in range(1, 4):
            a1[h][k - 1].wait_recv()
            forward(h, (z - k + 4) % 4)

    a3 = ([], [])

    def swap_features(h):
        for k in range(4):
            if k == 0:
                a2_local(h, i).wait()
            else:
                a2_copy(h, (i + k) % 4, k).wait_recv()
            piece = hblk.at[rows(h, (i - k + 4) % 4), mine]
            cp = remote(piece, piece, a3s.at[h, k], a3r.at[h, k], to_sib)
            cp.start()
            a3[h].append(cp)
        for cp in a3[h]:
            cp.wait_recv()

    def partial_logits(h):
        x = hblk[pl.ds(h * group, group), :]

        @pl.loop(0, voc // 256)
        def _(t):
            col = pl.ds(pl.multiple_of(t * 256, 256), 256)
            part[h, :, col] = jnp.dot(x, head_v[:, col], preferred_element_type=F32)

    lo, hi = pl.ds(0, quart), pl.ds(quart, quart)
    b = ([], [])

    def send_b(h, src, dst, to):
        n = len(b[h])
        cp = remote(src, dst, bs.at[h, n], br.at[h, n], to)
        cp.start()
        b[h].append(cp)

    def p_lo(h, block):
        return part.at[h, cut(block, 0, quart), :]

    def p_hi(h, block):
        return part.at[h, cut(block, quart, quart), :]

    def sum_start(h):
        send_b(h, p_lo(h, nd), relay.at[h, 0], to_x)
        send_b(h, p_hi(h, nd), relay.at[h, 1], to_y)
        send_b(h, p_lo(h, nx), got.at[h, 0, lo, :], to_x)
        send_b(h, p_hi(h, ny), got.at[h, 1, hi, :], to_y)

    def sum_relay(h):
        b[h][0].wait_recv()
        p_lo(h, ny)[...] = p_lo(h, ny)[...] + relay[h, 0]
        send_b(h, p_lo(h, ny), got.at[h, 1, lo, :], to_y)
        b[h][1].wait_recv()
        p_hi(h, nx)[...] = p_hi(h, nx)[...] + relay[h, 1]
        send_b(h, p_hi(h, nx), got.at[h, 0, hi, :], to_x)

    def teacher_rows(h):
        return tea_v[pl.ds(h * half, half), :].astype(F32)

    st = ([], [])

    def stats_start(h):
        for n in (2, 3, 4, 5):
            b[h][n].wait_recv()
        logits = part[h, cut(i), :] + got[h, 0] + got[h, 1]
        logits_v[h] = logits
        m = jnp.max(logits, axis=1, keepdims=True)
        e = jnp.exp(logits - m)
        s = jnp.sum(e, axis=1, keepdims=True)
        w = jnp.sum(e * (logits - teacher_rows(h)), axis=1, keepdims=True)
        lane = lax.broadcasted_iota(jnp.int32, (half, tok), 1)
        packed = jnp.where(lane == 0, m, jnp.where(lane == 1, s, w))
        packed = jnp.concatenate([packed, packed], axis=0)
        stat_v[h, j] = jnp.swapaxes(packed, 0, 1)[0:8, :]
        for k in range(1, 8):
            cp = remote(
                stat_v.at[h, j], stat_v.at[h, j], ss.at[h, k], sr.at[h, k],
                {"vocab": (j + k) % 8},
            )
            cp.start()
            st[h].append(cp)

    def gradient(h):
        for cp in st[h]:
            cp.wait_recv()
        stats = stat_v[h]
        tops = stats[:, 0, :]
        top = jnp.max(tops, axis=0, keepdims=True)
        scale = jnp.exp(tops - top)
        total = jnp.sum(stats[:, 1, :] * scale, axis=0, keepdims=True)
        weighted = jnp.sum(stats[:, 2, :] * scale, axis=0, keepdims=True)
        sub = lax.broadcasted_iota(jnp.int32, (tok, tok), 0)
        table = jnp.where(sub == 0, top, jnp.where(sub == 1, total, jnp.where(
            sub == 2, weighted / total, jnp.where(
                sub == 3, ids_v[...].astype(F32), mask_v[...].astype(F32)))))
        table = jnp.swapaxes(table, 0, 1)[h * half:(h + 1) * half, :]
        logits = logits_v[h]
        prob = jnp.exp(logits - table[:, 0:1]) / table[:, 1:2]
        gap = logits - teacher_rows(h)
        ids = table[:, 3:4].astype(jnp.int32) - j * voc
        onehot = (lax.broadcasted_iota(jnp.int32, (half, voc), 1) == ids).astype(F32)
        lg = table[:, 4:5] * (prob * (gap - table[:, 2:3]) + anchor_weight * (prob - onehot))
        lgb[rows(h, i), :] = lg.astype(BF16)

    cc = ([], [])

    def send_c(h, block, begin, to):
        n = len(cc[h])
        piece = lgb.at[rows(h, block, begin, quart), :]
        cp = remote(piece, piece, cs.at[h, n], cr.at[h, n], to)
        cp.start()
        cc[h].append(cp)

    def gather_start(h):
        send_c(h, i, 0, to_x)
        send_c(h, i, quart, to_y)
        send_c(h, i, quart, to_x)
        send_c(h, i, 0, to_y)
        cp = pltpu.make_async_copy(
            lgb.at[rows(h, i), :], lg_out.at[pl.ds(h * half, half), :], wsem.at[4 + h])
        cp.start()
        return cp

    def gather_relay(h):
        cc[h][0].wait_recv()
        send_c(h, nx, 0, to_y)
        cc[h][1].wait_recv()
        send_c(h, ny, quart, to_x)

    ecps = []

    def hidden_part(h):
        for n in (2, 3, 4, 5):
            cc[h][n].wait_recv()
        g = lgb[pl.ds(h * group, group), :]
        sib_out[h] = jnp.dot(g, head_t[:, other], preferred_element_type=F32).astype(BF16)
        cp = remote(sib_out.at[h], sib_in.at[h], es.at[h], er.at[h], to_sib)
        cp.start()
        ecps.append(cp)
        hown[h] = jnp.dot(g, head_t[:, mine], preferred_element_type=F32)

    def d2_copy(h, r, shift, zt):
        return remote(
            d1_in.at[h, r], d2_in.at[h, shift], d2s.at[h, shift], d2r.at[h, shift],
            {"vocab": zt * 2 + c},
        )

    def d2_send(h, r):
        zt = rel[r]
        shift = (zt - z + 4) % 4

        @pl.when(shift != 0)
        def _():
            d2_copy(h, r, shift, zt).start()

        @pl.when(shift == 0)
        def _():
            d2_in[h, 0] = d1_in[h, r]

    d1 = ([], [])

    def scatter_start(h):
        ecps[h].wait_recv()
        d1_out[h] = (hown[h] + sib_in[h].astype(F32)).astype(BF16)
        for r in (3, 1, 2):
            cp = remote(
                d1_out.at[h, cut(rel[r]), :], d1_in.at[h, r], d1s.at[h, r], d1r.at[h, r], to_rel[r])
            cp.start()
            d1[h].append(cp)
        d1_in[h, 0] = d1_out[h, cut(i), :]
        d2_send(h, 0)

    def scatter_relay(h):
        for n, r in ((1, 1), (2, 2), (0, 3)):
            d1[h][n].wait_recv()
            d2_send(h, r)

    def scatter_end(h):
        for k in range(1, 4):
            d2_copy(h, 0, k, (z + k) % 4).wait_recv()
        acc = d2_in[h, 0].astype(F32)
        for k in range(1, 4):
            acc = acc + d2_in[h, k].astype(F32)
        hg_v[pl.ds(h * half, half), :] = acc
        piece = pl.ds(h * half, half)
        cp = pltpu.make_async_copy(hg_v.at[piece, :], hg_out.at[piece, :], wsem.at[6 + h])
        cp.start()
        return cp

    wcps = []
    quarter = width // 4

    def weight_part(t):
        band = pl.ds(t * quarter, quarter)

        @pl.loop(0, voc // 256)
        def _(u):
            col = pl.ds(pl.multiple_of(u * 256, 256), 256)
            wg_v[band, col] = jnp.dot(
                hid_t[band, :], lgb[:, col], preferred_element_type=F32).astype(BF16)

        cp = pltpu.make_async_copy(wg_v.at[band, :], wg_out.at[band, :], wsem.at[t])
        cp.start()
        wcps.append(cp)

    send_a1(0)
    cp_hid.wait()
    for cp in a1[0]:
        cp.wait_send()
    send_a1(1)
    forward_all(0)
    swap_features(0)
    cp_head.wait()
    partial_logits(0)
    sum_start(0)
    forward_all(1)
    tcps = []
    for k in range(1, 8):
        jt = (j + k) % 8
        cp = remote(
            tea_ref.at[:, pl.ds(pl.multiple_of(jt * voc, voc), voc)], tea_v.at[own_trow, :],
            ts.at[k], tr.at[k], {"vocab": jt},
        )
        cp.start()
        tcps.append(cp)
    sum_relay(0)
    swap_features(1)
    partial_logits(1)
    sum_start(1)

    @pl.loop(0, width // 256)
    def _(t):
        band = pl.ds(pl.multiple_of(t * 256, 256), 256)
        hid_t[band, :] = jnp.swapaxes(hblk[:, band], 0, 1)

    cp_tea.wait()
    for cp in tcps:
        cp.wait_recv()
    cp_ids.wait()
    cp_mask.wait()
    stats_start(0)
    sum_relay(1)
    gradient(0)
    out_cps = [gather_start(0)]

    @pl.loop(0, width // 256)
    def _(t):
        band = pl.ds(pl.multiple_of(t * 256, 256), 256)
        head_t[:, band] = jnp.swapaxes(head_v[band, :], 0, 1)

    stats_start(1)
    gather_relay(0)
    gradient(1)
    out_cps.append(gather_start(1))
    hidden_part(0)
    gather_relay(1)
    scatter_start(0)
    hidden_part(1)
    scatter_relay(0)
    scatter_start(1)
    weight_part(0)
    weight_part(1)
    scatter_relay(1)
    weight_part(2)
    weight_part(3)
    out_cps.append(scatter_end(0))
    out_cps.append(scatter_end(1))

    for cp in a1[1] + tcps + ecps:
        cp.wait_send()
    for h in range(2):
        for cp in a3[h] + b[h] + st[h] + cc[h] + d1[h]:
            cp.wait_send()
        for k in range(1, 4):
            a2_copy(h, (i + k) % 4, k).wait_send()
            d2_copy(h, 0, k, (z + k) % 4).wait_send()
    for cp in wcps + out_cps:
        cp.wait()


def fused(hidden_states, teacher_logprob, head_weight, token_ids, padding_mask):
    tok, feat = hidden_states.shape
    width, voc = head_weight.shape
    trow = teacher_logprob.shape[0]
    half = tok // 2
    any_spec = pl.BlockSpec(memory_space=pl.ANY)
    dma = pltpu.SemaphoreType.DMA
    return pl.pallas_call(
        kernel,
        out_shape=(
            jax.ShapeDtypeStruct((tok, voc), BF16),
            jax.ShapeDtypeStruct((tok, feat), F32),
            jax.ShapeDtypeStruct((width, voc), BF16),
        ),
        in_specs=[any_spec] * 5,
        out_specs=[any_spec] * 3,
        scratch_shapes=[
            pltpu.VMEM((width, voc), BF16),
            pltpu.VMEM((voc, width), BF16),
            pltpu.VMEM((4, tok, feat), BF16),
            pltpu.VMEM((4 * tok, width), BF16),
            pltpu.VMEM((width, 4 * tok), BF16),
            pltpu.VMEM((8 * trow, voc), BF16),
            pltpu.VMEM((1, tok), jnp.int32),
            pltpu.VMEM((1, tok), jnp.int32),
            pltpu.VMEM((2, 4 * half, voc), F32),
            pltpu.VMEM((2, 2, half // 2, voc), F32),
            pltpu.VMEM((2, 2, half, voc), F32),
            pltpu.VMEM((2, half, voc), F32),
            pltpu.VMEM((2, 8, 8, tok), F32),
            pltpu.VMEM((4 * tok, voc), BF16),
            pltpu.VMEM((2, 4 * half, feat), F32),
            pltpu.VMEM((2, 4 * half, feat), BF16),
            pltpu.VMEM((2, 4 * half, feat), BF16),
            pltpu.VMEM((2, 4 * half, feat), BF16),
            pltpu.VMEM((2, 4, half, feat), BF16),
            pltpu.VMEM((2, 4, half, feat), BF16),
            pltpu.VMEM((width, voc), BF16),
            pltpu.VMEM((tok, feat), F32),
            dma((7,)), dma((2, 4)), dma((2, 4)), dma((2, 4)), dma((2, 4)), dma((2, 4)), dma((2, 4)),
            dma((8,)), dma((8,)), dma((2, 6)), dma((2, 6)), dma((2, 8)), dma((2, 8)),
            dma((2, 6)), dma((2, 6)), dma((2,)), dma((2,)), dma((2, 4)), dma((2, 4)),
            dma((2, 4)), dma((2, 4)), dma((8,)),
        ],
        compiler_params=pltpu.CompilerParams(
            collective_id=0, has_side_effects=True, vmem_limit_bytes=62 * 1024 * 1024
        ),
        cost_estimate=pl.CostEstimate(
            flops=6 * 4 * tok * width * voc, bytes_accessed=6 * width * voc,
            transcendentals=2 * tok * voc,
        ),
    )(
        hidden_states, teacher_logprob, head_weight,
        token_ids.reshape(1, tok), padding_mask.reshape(1, tok),
    )


def gathered(n_dp, n_vocab, hidden_states, teacher_logprob, head_weight, token_ids, padding_mask):
    voc = head_weight.shape[1]
    full = lax.all_gather(hidden_states, "vocab", axis=1, tiled=True)
    block = lax.all_to_all(full, "dp", split_axis=1, concat_axis=0, tiled=True)
    teacher = lax.all_to_all(teacher_logprob, "vocab", split_axis=1, concat_axis=0, tiled=True)
    part = jnp.dot(block, head_weight, preferred_element_type=F32)
    logits = lax.psum_scatter(part, "dp", scatter_dimension=0, tiled=True)
    gap = logits - teacher.astype(F32)
    top = lax.pmax(jnp.max(logits, axis=1), "vocab")
    expo = jnp.exp(logits - top[:, None])
    total, weighted = lax.psum((jnp.sum(expo, axis=1), jnp.sum(expo * gap, axis=1)), "vocab")
    columns = lax.axis_index("vocab") * voc + jnp.arange(voc, dtype=jnp.int32)
    onehot = (columns[None, :] == token_ids[:, None]).astype(F32)
    prob = expo / total[:, None]
    keep = padding_mask.astype(F32)[:, None]
    logit_grad = (
        keep * (prob * (gap - (weighted / total)[:, None]) + anchor_weight * (prob - onehot))
    ).astype(BF16)
    every = lax.all_gather(logit_grad, "dp", axis=0, tiled=True)
    head_grad = lax.dot_general(
        block, every, (((0,), (0,)), ((), ())), preferred_element_type=F32).astype(BF16)
    back = lax.dot_general(
        every, head_weight, (((1,), (1,)), ((), ())), preferred_element_type=F32)
    back = lax.all_to_all(back, "dp", split_axis=0, concat_axis=1, tiled=True)
    hidden_grad = lax.psum_scatter(back, "vocab", scatter_dimension=1, tiled=True)
    return (logit_grad, hidden_grad, head_grad)


def solution(mesh):
    in_specs = (P("dp", "vocab"), P(("dp", "vocab"), None), P("dp", "vocab"), P("dp"), P("dp"))
    out_specs = (P("dp", "vocab"), P("dp", "vocab"), P("dp", "vocab"))
    n_dp, n_vocab = mesh.shape["dp"], mesh.shape["vocab"]
    body = fused if (n_dp, n_vocab) == (4, 8) else functools.partial(gathered, n_dp, n_vocab)
    return jax.shard_map(body, mesh=mesh, in_specs=in_specs, out_specs=out_specs, check_vma=False)
```

```python
import functools
import jax
import jax.numpy as jnp
from jax import lax
from jax.experimental import pallas as pl
from jax.experimental.pallas import tpu as pltpu
from jax.sharding import PartitionSpec as P

anchor_weight = 0.25
MESH = pl.DeviceIdType.MESH
F32 = jnp.float32
BF16 = jnp.bfloat16


def kernel(
    hid_ref, tea_ref, head_ref, ids_ref, mask_ref,
    lg_out, hg_out, wg_out,
    head_v, head_t, zbuf, hblk, hid_t, tea_v, ids_v, mask_v, part, relay, got, logits_v, stat_v,
    lgb, hown, sib_out, sib_in, d1_out, d1_in, d2_in, wg_v, hg_v,
    loc_sem, a1s, a1r, a2s, a2r, a3s, a3r, ts, tr, bs, br, ss, sr, cs, cr,
    es, er, d1s, d1r, d2s, d2r, wsem,
):
    tok, feat = hid_ref.shape
    width, voc = head_ref.shape
    half = tok // 2
    quart = half // 2
    group = 4 * half
    trow = tea_ref.shape[0]
    i, j = lax.axis_index("dp"), lax.axis_index("vocab")
    z, c = j // 2, j % 2
    sib = z * 2 + (1 - c)
    nx = i + 1 - 2 * (i % 2)
    ny = (i + 2) % 4
    nd = 3 - i
    rel = (i, nx, ny, nd)
    to_x, to_y, to_d = {"dp": nx}, {"dp": ny}, {"dp": nd}
    to_rel = (None, to_x, to_y, to_d)
    to_sib = {"vocab": sib}

    def remote(src, dst, ssem, rsem, to):
        return pltpu.make_async_remote_copy(
            src_ref=src, dst_ref=dst, send_sem=ssem, recv_sem=rsem,
            device_id=to, device_id_type=MESH,
        )

    def cut(block, begin=0, size=None):
        size = half if size is None else size
        return pl.ds(pl.multiple_of(block * half + begin, 16), size)

    def rows(h, block, begin=0, size=None):
        return cut(h * 4 + block, begin, size)

    mine = pl.ds(pl.multiple_of(c * feat, feat), feat)
    other = pl.ds(pl.multiple_of((1 - c) * feat, feat), feat)

    own_cols = pl.ds(pl.multiple_of(j * voc, voc), voc)
    own_trow = pl.ds(pl.multiple_of(j * trow, trow), trow)
    cp_hid = pltpu.make_async_copy(hid_ref, zbuf.at[z], loc_sem.at[0])
    cp_head = pltpu.make_async_copy(head_ref, head_v, loc_sem.at[1])
    cp_tea = pltpu.make_async_copy(tea_ref.at[:, own_cols], tea_v.at[own_trow, :], loc_sem.at[2])
    cp_ids = pltpu.make_async_copy(ids_ref, ids_v, loc_sem.at[3])
    cp_mask = pltpu.make_async_copy(mask_ref, mask_v, loc_sem.at[4])
    for cp in (cp_hid, cp_head, cp_tea, cp_ids, cp_mask):
        cp.start()

    barrier = pltpu.get_barrier_semaphore()
    for k in range(1, 4):
        pl.semaphore_signal(barrier, inc=1, device_id={"dp": (i + k) % 4}, device_id_type=MESH)
    for k in range(1, 8):
        pl.semaphore_signal(barrier, inc=1, device_id={"vocab": (j + k) % 8}, device_id_type=MESH)
    pl.semaphore_wait(barrier, 10)

    a1 = ([], [])

    def send_a1(h):
        piece = pl.ds(h * half, half)
        for k in range(1, 4):
            cp = remote(
                hid_ref.at[piece, :], zbuf.at[z, piece, :], a1s.at[h, k], a1r.at[h, k],
                {"vocab": ((z + k) % 4) * 2 + c},
            )
            cp.start()
            a1[h].append(cp)

    def a2_copy(h, zs, shift):
        return remote(
            zbuf.at[zs, pl.ds(h * half, half), :], hblk.at[rows(h, i), mine],
            a2s.at[h, shift], a2r.at[h, shift], {"dp": zs},
        )

    def a2_local(h, zs):
        return pltpu.make_async_copy(
            zbuf.at[zs, pl.ds(h * half, half), :], hblk.at[rows(h, i), mine], loc_sem.at[5 + h]
        )

    def forward(h, zs):
        shift = (zs - i + 4) % 4

        @pl.when(shift != 0)
        def _():
            a2_copy(h, zs, shift).start()

        @pl.when(shift == 0)
        def _():
            a2_local(h, zs).start()

    def forward_rest(h):
        for k in range(1, 4):
            a1[h][k - 1].wait_recv()
            forward(h, (z - k + 4) % 4)

    a3 = ([], [])

    def swap_start(h):
        for k in range(4):
            if k == 0:
                a2_local(h, i).wait()
            else:
                a2_copy(h, (i + k) % 4, k).wait_recv()
            piece = hblk.at[rows(h, (i - k + 4) % 4), mine]
            cp = remote(piece, piece, a3s.at[h, k], a3r.at[h, k], to_sib)
            cp.start()
            a3[h].append(cp)

    def swap_end(h):
        for cp in a3[h]:
            cp.wait_recv()

    def partial_logits(h):
        x = hblk[pl.ds(h * group, group), :]

        @pl.loop(0, voc // 256)
        def _(t):
            col = pl.ds(pl.multiple_of(t * 256, 256), 256)
            part[h, :, col] = jnp.dot(x, head_v[:, col], preferred_element_type=F32)

    lo, hi = pl.ds(0, quart), pl.ds(quart, quart)
    b = ([], [])

    def send_b(h, src, dst, to):
        n = len(b[h])
        cp = remote(src, dst, bs.at[h, n], br.at[h, n], to)
        cp.start()
        b[h].append(cp)

    def p_lo(h, block):
        return part.at[h, cut(block, 0, quart), :]

    def p_hi(h, block):
        return part.at[h, cut(block, quart, quart), :]

    def sum_start(h):
        send_b(h, p_lo(h, nd), relay.at[h, 0], to_x)
        send_b(h, p_hi(h, nd), relay.at[h, 1], to_y)
        send_b(h, p_lo(h, nx), got.at[h, 0, lo, :], to_x)
        send_b(h, p_hi(h, ny), got.at[h, 1, hi, :], to_y)

    def sum_relay(h):
        b[h][0].wait_recv()
        p_lo(h, ny)[...] = p_lo(h, ny)[...] + relay[h, 0]
        send_b(h, p_lo(h, ny), got.at[h, 1, lo, :], to_y)
        b[h][1].wait_recv()
        p_hi(h, nx)[...] = p_hi(h, nx)[...] + relay[h, 1]
        send_b(h, p_hi(h, nx), got.at[h, 0, hi, :], to_x)

    def teacher_rows(h):
        return tea_v[pl.ds(h * half, half), :].astype(F32)

    st = ([], [])

    def stats_start(h):
        for n in (2, 3, 4, 5):
            b[h][n].wait_recv()
        logits = part[h, cut(i), :] + got[h, 0] + got[h, 1]
        logits_v[h] = logits
        m = jnp.max(logits, axis=1, keepdims=True)
        e = jnp.exp(logits - m)
        s = jnp.sum(e, axis=1, keepdims=True)
        w = jnp.sum(e * (logits - teacher_rows(h)), axis=1, keepdims=True)
        lane = lax.broadcasted_iota(jnp.int32, (half, tok), 1)
        packed = jnp.where(lane == 0, m, jnp.where(lane == 1, s, w))
        packed = jnp.concatenate([packed, packed], axis=0)
        stat_v[h, j] = jnp.swapaxes(packed, 0, 1)[0:8, :]
        for k in range(1, 8):
            cp = remote(
                stat_v.at[h, j], stat_v.at[h, j], ss.at[h, k], sr.at[h, k],
                {"vocab": (j + k) % 8},
            )
            cp.start()
            st[h].append(cp)

    def gradient(h):
        for cp in st[h]:
            cp.wait_recv()
        stats = stat_v[h]
        tops = stats[:, 0, :]
        top = jnp.max(tops, axis=0, keepdims=True)
        scale = jnp.exp(tops - top)
        total = jnp.sum(stats[:, 1, :] * scale, axis=0, keepdims=True)
        weighted = jnp.sum(stats[:, 2, :] * scale, axis=0, keepdims=True)
        sub = lax.broadcasted_iota(jnp.int32, (tok, tok), 0)
        table = jnp.where(sub == 0, top, jnp.where(sub == 1, total, jnp.where(
            sub == 2, weighted / total, jnp.where(
                sub == 3, ids_v[...].astype(F32), mask_v[...].astype(F32)))))
        table = jnp.swapaxes(table, 0, 1)[h * half:(h + 1) * half, :]
        logits = logits_v[h]
        prob = jnp.exp(logits - table[:, 0:1]) / table[:, 1:2]
        gap = logits - teacher_rows(h)
        ids = table[:, 3:4].astype(jnp.int32) - j * voc
        onehot = (lax.broadcasted_iota(jnp.int32, (half, voc), 1) == ids).astype(F32)
        lg = table[:, 4:5] * (prob * (gap - table[:, 2:3]) + anchor_weight * (prob - onehot))
        lgb[rows(h, i), :] = lg.astype(BF16)

    cc = ([], [])

    def send_c(h, block, begin, to):
        n = len(cc[h])
        piece = lgb.at[rows(h, block, begin, quart), :]
        cp = remote(piece, piece, cs.at[h, n], cr.at[h, n], to)
        cp.start()
        cc[h].append(cp)

    def gather_start(h):
        send_c(h, i, 0, to_x)
        send_c(h, i, quart, to_y)
        send_c(h, i, quart, to_x)
        send_c(h, i, 0, to_y)
        cp = pltpu.make_async_copy(
            lgb.at[rows(h, i), :], lg_out.at[pl.ds(h * half, half), :], wsem.at[4 + h])
        cp.start()
        return cp

    def gather_relay(h):
        cc[h][0].wait_recv()
        send_c(h, nx, 0, to_y)
        cc[h][1].wait_recv()
        send_c(h, ny, quart, to_x)

    ecps = []

    def hidden_part(h):
        for n in (2, 3, 4, 5):
            cc[h][n].wait_recv()
        g = lgb[pl.ds(h * group, group), :]
        sib_out[h] = jnp.dot(g, head_t[:, other], preferred_element_type=F32).astype(BF16)
        cp = remote(sib_out.at[h], sib_in.at[h], es.at[h], er.at[h], to_sib)
        cp.start()
        ecps.append(cp)
        hown[h] = jnp.dot(g, head_t[:, mine], preferred_element_type=F32)

    def d2_copy(h, r, shift, zt):
        return remote(
            d1_in.at[h, r], d2_in.at[h, shift], d2s.at[h, shift], d2r.at[h, shift],
            {"vocab": zt * 2 + c},
        )

    def d2_send(h, r):
        zt = rel[r]
        shift = (zt - z + 4) % 4

        @pl.when(shift != 0)
        def _():
            d2_copy(h, r, shift, zt).start()

        @pl.when(shift == 0)
        def _():
            d2_in[h, 0] = d1_in[h, r]

    d1 = ([], [])

    def scatter_start(h):
        ecps[h].wait_recv()
        d1_out[h] = (hown[h] + sib_in[h].astype(F32)).astype(BF16)
        for r in (3, 1, 2):
            cp = remote(
                d1_out.at[h, cut(rel[r]), :], d1_in.at[h, r], d1s.at[h, r], d1r.at[h, r], to_rel[r])
            cp.start()
            d1[h].append(cp)
        d1_in[h, 0] = d1_out[h, cut(i), :]
        d2_send(h, 0)

    def scatter_relay(h):
        for n, r in ((1, 1), (2, 2), (0, 3)):
            d1[h][n].wait_recv()
            d2_send(h, r)

    def scatter_end(h):
        for k in range(1, 4):
            d2_copy(h, 0, k, (z + k) % 4).wait_recv()
        acc = d2_in[h, 0].astype(F32)
        for k in range(1, 4):
            acc = acc + d2_in[h, k].astype(F32)
        hg_v[pl.ds(h * half, half), :] = acc
        piece = pl.ds(h * half, half)
        cp = pltpu.make_async_copy(hg_v.at[piece, :], hg_out.at[piece, :], wsem.at[6 + h])
        cp.start()
        return cp

    wcps = []
    quarter = width // 4

    def weight_part(t):
        band = pl.ds(t * quarter, quarter)

        @pl.loop(0, voc // 256)
        def _(u):
            col = pl.ds(pl.multiple_of(u * 256, 256), 256)
            wg_v[band, col] = jnp.dot(
                hid_t[band, :], lgb[:, col], preferred_element_type=F32).astype(BF16)

        cp = pltpu.make_async_copy(wg_v.at[band, :], wg_out.at[band, :], wsem.at[t])
        cp.start()
        wcps.append(cp)

    def turn_head(t):
        band = pl.ds(t * quarter, quarter)
        head_t[:, band] = jnp.swapaxes(head_v[band, :], 0, 1)

    def turn_hidden(h):
        group_rows = pl.ds(h * group, group)

        @pl.loop(0, width // 256)
        def _(t):
            band = pl.ds(pl.multiple_of(t * 256, 256), 256)
            hid_t[band, group_rows] = jnp.swapaxes(hblk[group_rows, band], 0, 1)

    send_a1(0)
    cp_hid.wait()
    forward(0, z)
    for cp in a1[0]:
        cp.wait_send()
    send_a1(1)
    cp_head.wait()
    turn_head(0)
    forward_rest(0)
    turn_head(1)
    swap_start(0)
    turn_head(2)
    swap_end(0)
    partial_logits(0)
    sum_start(0)
    forward(1, z)
    forward_rest(1)
    tcps = []
    for k in range(1, 8):
        jt = (j + k) % 8
        cp = remote(
            tea_ref.at[:, pl.ds(pl.multiple_of(jt * voc, voc), voc)], tea_v.at[own_trow, :],
            ts.at[k], tr.at[k], {"vocab": jt},
        )
        cp.start()
        tcps.append(cp)
    turn_head(3)
    sum_relay(0)
    swap_start(1)
    swap_end(1)
    partial_logits(1)
    sum_start(1)
    cp_tea.wait()
    for cp in tcps:
        cp.wait_recv()
    cp_ids.wait()
    cp_mask.wait()
    stats_start(0)
    turn_hidden(0)
    gradient(0)
    sum_relay(1)
    out_cps = [gather_start(0)]
    turn_hidden(1)
    gather_relay(0)
    stats_start(1)
    gradient(1)
    out_cps.append(gather_start(1))
    hidden_part(0)
    gather_relay(1)
    scatter_start(0)
    hidden_part(1)
    scatter_relay(0)
    scatter_start(1)
    weight_part(0)
    weight_part(1)
    scatter_relay(1)
    weight_part(2)
    weight_part(3)
    out_cps.append(scatter_end(0))
    out_cps.append(scatter_end(1))

    for cp in a1[1] + tcps + ecps:
        cp.wait_send()
    for h in range(2):
        for cp in a3[h] + b[h] + st[h] + cc[h] + d1[h]:
            cp.wait_send()
        for k in range(1, 4):
            a2_copy(h, (i + k) % 4, k).wait_send()
            d2_copy(h, 0, k, (z + k) % 4).wait_send()
    for cp in wcps + out_cps:
        cp.wait()


def store(lg_ref, hg_ref, wg_ref, lg_out, hg_out, wg_out, sem):
    copies = [
        pltpu.make_async_copy(lg_ref, lg_out, sem.at[4]),
        pltpu.make_async_copy(hg_ref, hg_out, sem.at[5]),
    ]
    quarter = wg_ref.shape[0] // 4
    for t in range(4):
        band = pl.ds(t * quarter, quarter)
        copies.append(pltpu.make_async_copy(wg_ref.at[band, :], wg_out.at[band, :], sem.at[t]))
    for cp in copies:
        cp.start()
    for cp in copies:
        cp.wait()


def fused(hidden_states, teacher_logprob, head_weight, token_ids, padding_mask):
    tok, feat = hidden_states.shape
    width, voc = head_weight.shape
    trow = teacher_logprob.shape[0]
    half = tok // 2
    any_spec = pl.BlockSpec(memory_space=pl.ANY)
    dma = pltpu.SemaphoreType.DMA
    held = pl.pallas_call(
        kernel,
        out_shape=(
            jax.ShapeDtypeStruct((tok, voc), BF16),
            jax.ShapeDtypeStruct((tok, feat), F32),
            jax.ShapeDtypeStruct((width, voc), BF16),
        ),
        in_specs=[pl.BlockSpec(memory_space=pltpu.HBM)] * 5,
        out_specs=[any_spec] * 3,
        scratch_shapes=[
            pltpu.VMEM((width, voc), BF16),
            pltpu.VMEM((voc, width), BF16),
            pltpu.VMEM((4, tok, feat), BF16),
            pltpu.VMEM((4 * tok, width), BF16),
            pltpu.VMEM((width, 4 * tok), BF16),
            pltpu.VMEM((8 * trow, voc), BF16),
            pltpu.VMEM((1, tok), jnp.int32),
            pltpu.VMEM((1, tok), jnp.int32),
            pltpu.VMEM((2, 4 * half, voc), F32),
            pltpu.VMEM((2, 2, half // 2, voc), F32),
            pltpu.VMEM((2, 2, half, voc), F32),
            pltpu.VMEM((2, half, voc), F32),
            pltpu.VMEM((2, 8, 8, tok), F32),
            pltpu.VMEM((4 * tok, voc), BF16),
            pltpu.VMEM((2, 4 * half, feat), F32),
            pltpu.VMEM((2, 4 * half, feat), BF16),
            pltpu.VMEM((2, 4 * half, feat), BF16),
            pltpu.VMEM((2, 4 * half, feat), BF16),
            pltpu.VMEM((2, 4, half, feat), BF16),
            pltpu.VMEM((2, 4, half, feat), BF16),
            pltpu.VMEM((width, voc), BF16),
            pltpu.VMEM((tok, feat), F32),
            dma((7,)), dma((2, 4)), dma((2, 4)), dma((2, 4)), dma((2, 4)), dma((2, 4)), dma((2, 4)),
            dma((8,)), dma((8,)), dma((2, 6)), dma((2, 6)), dma((2, 8)), dma((2, 8)),
            dma((2, 6)), dma((2, 6)), dma((2,)), dma((2,)), dma((2, 4)), dma((2, 4)),
            dma((2, 4)), dma((2, 4)), dma((8,)),
        ],
        compiler_params=pltpu.CompilerParams(
            collective_id=0, has_side_effects=True, vmem_limit_bytes=62 * 1024 * 1024
        ),
        cost_estimate=pl.CostEstimate(
            flops=6 * 4 * tok * width * voc, bytes_accessed=6 * width * voc,
            transcendentals=2 * tok * voc,
        ),
    )(
        hidden_states, teacher_logprob, head_weight,
        token_ids.reshape(1, tok), padding_mask.reshape(1, tok),
    )
    return pl.pallas_call(
        store,
        out_shape=tuple(jax.ShapeDtypeStruct(x.shape, x.dtype) for x in held),
        in_specs=[any_spec] * 3,
        out_specs=[pl.BlockSpec(memory_space=pltpu.HBM)] * 3,
        scratch_shapes=[dma((6,))],
        compiler_params=pltpu.CompilerParams(vmem_limit_bytes=62 * 1024 * 1024),
    )(*held)


def gathered(n_dp, n_vocab, hidden_states, teacher_logprob, head_weight, token_ids, padding_mask):
    voc = head_weight.shape[1]
    full = lax.all_gather(hidden_states, "vocab", axis=1, tiled=True)
    block = lax.all_to_all(full, "dp", split_axis=1, concat_axis=0, tiled=True)
    teacher = lax.all_to_all(teacher_logprob, "vocab", split_axis=1, concat_axis=0, tiled=True)
    part = jnp.dot(block, head_weight, preferred_element_type=F32)
    logits = lax.psum_scatter(part, "dp", scatter_dimension=0, tiled=True)
    gap = logits - teacher.astype(F32)
    top = lax.pmax(jnp.max(logits, axis=1), "vocab")
    expo = jnp.exp(logits - top[:, None])
    total, weighted = lax.psum((jnp.sum(expo, axis=1), jnp.sum(expo * gap, axis=1)), "vocab")
    columns = lax.axis_index("vocab") * voc + jnp.arange(voc, dtype=jnp.int32)
    onehot = (columns[None, :] == token_ids[:, None]).astype(F32)
    prob = expo / total[:, None]
    keep = padding_mask.astype(F32)[:, None]
    logit_grad = (
        keep * (prob * (gap - (weighted / total)[:, None]) + anchor_weight * (prob - onehot))
    ).astype(BF16)
    every = lax.all_gather(logit_grad, "dp", axis=0, tiled=True)
    head_grad = lax.dot_general(
        block, every, (((0,), (0,)), ((), ())), preferred_element_type=F32).astype(BF16)
    back = lax.dot_general(
        every, head_weight, (((1,), (1,)), ((), ())), preferred_element_type=F32)
    back = lax.all_to_all(back, "dp", split_axis=0, concat_axis=1, tiled=True)
    hidden_grad = lax.psum_scatter(back, "vocab", scatter_dimension=1, tiled=True)
    return (logit_grad, hidden_grad, head_grad)


def solution(mesh):
    in_specs = (P("dp", "vocab"), P(("dp", "vocab"), None), P("dp", "vocab"), P("dp"), P("dp"))
    out_specs = (P("dp", "vocab"), P("dp", "vocab"), P("dp", "vocab"))
    n_dp, n_vocab = mesh.shape["dp"], mesh.shape["vocab"]
    body = fused if (n_dp, n_vocab) == (4, 8) else functools.partial(gathered, n_dp, n_vocab)
    return jax.shard_map(body, mesh=mesh, in_specs=in_specs, out_specs=out_specs, check_vma=False)
```

```python
import functools
import jax
import jax.numpy as jnp
from jax import lax
from jax.experimental import pallas as pl
from jax.experimental.pallas import tpu as pltpu
from jax.sharding import PartitionSpec as P

anchor_weight = 0.25
MESH = pl.DeviceIdType.MESH
F32 = jnp.float32
BF16 = jnp.bfloat16


def kernel(
    hid_ref, tea_ref, head_ref, ids_ref, mask_ref,
    lg_out, hg_out, wg_out,
    head_v, head_t, zbuf, hblk, hid_t, tea_src, tea_v, ids_v, mask_v, part, relay, got, logits_v, stat_v,
    lgb, hown, sib_out, sib_in, d1_out, d1_in, d2_in, wg_v, hg_v,
    loc_sem, a1s, a1r, a2s, a2r, a3s, a3r, ts, tr, bs, br, ss, sr, cs, cr,
    es, er, d1s, d1r, d2s, d2r, wsem,
):
    tok, feat = hid_ref.shape
    width, voc = head_ref.shape
    half = tok // 2
    quart = half // 2
    group = 4 * half
    trow = tea_ref.shape[0]
    i, j = lax.axis_index("dp"), lax.axis_index("vocab")
    z, c = j // 2, j % 2
    sib = z * 2 + (1 - c)
    nx = i + 1 - 2 * (i % 2)
    ny = (i + 2) % 4
    nd = 3 - i
    rel = (i, nx, ny, nd)
    to_x, to_y, to_d = {"dp": nx}, {"dp": ny}, {"dp": nd}
    to_rel = (None, to_x, to_y, to_d)
    to_sib = {"vocab": sib}

    def remote(src, dst, ssem, rsem, to):
        return pltpu.make_async_remote_copy(
            src_ref=src, dst_ref=dst, send_sem=ssem, recv_sem=rsem,
            device_id=to, device_id_type=MESH,
        )

    def cut(block, begin=0, size=None):
        size = half if size is None else size
        return pl.ds(pl.multiple_of(block * half + begin, 16), size)

    def rows(h, block, begin=0, size=None):
        return cut(h * 4 + block, begin, size)

    mine = pl.ds(pl.multiple_of(c * feat, feat), feat)
    other = pl.ds(pl.multiple_of((1 - c) * feat, feat), feat)

    own_cols = pl.ds(pl.multiple_of(j * voc, voc), voc)
    own_trow = pl.ds(pl.multiple_of(j * trow, trow), trow)
    cp_hid = pltpu.make_async_copy(hid_ref, zbuf.at[z], loc_sem.at[0])
    cp_head = pltpu.make_async_copy(head_ref, head_v, loc_sem.at[1])
    cp_tea = pltpu.make_async_copy(tea_ref, tea_src, loc_sem.at[2])
    cp_ids = pltpu.make_async_copy(ids_ref, ids_v, loc_sem.at[3])
    cp_mask = pltpu.make_async_copy(mask_ref, mask_v, loc_sem.at[4])
    for cp in (cp_hid, cp_head, cp_tea, cp_ids, cp_mask):
        cp.start()

    barrier = pltpu.get_barrier_semaphore()
    for k in range(1, 4):
        pl.semaphore_signal(barrier, inc=1, device_id={"dp": (i + k) % 4}, device_id_type=MESH)
    for k in range(1, 8):
        pl.semaphore_signal(barrier, inc=1, device_id={"vocab": (j + k) % 8}, device_id_type=MESH)
    pl.semaphore_wait(barrier, 10)

    a1 = ([], [])

    def send_a1(h):
        piece = pl.ds(h * half, half)
        for k in range(1, 4):
            cp = remote(
                zbuf.at[z, piece, :], zbuf.at[z, piece, :], a1s.at[h, k], a1r.at[h, k],
                {"vocab": ((z + k) % 4) * 2 + c},
            )
            cp.start()
            a1[h].append(cp)

    def a2_copy(h, zs, shift):
        return remote(
            zbuf.at[zs, pl.ds(h * half, half), :], hblk.at[rows(h, i), mine],
            a2s.at[h, shift], a2r.at[h, shift], {"dp": zs},
        )

    def forward(h, zs):
        shift = (zs - i + 4) % 4

        @pl.when(shift != 0)
        def _():
            a2_copy(h, zs, shift).start()

        @pl.when(shift == 0)
        def _():
            hblk[rows(h, i), mine] = zbuf[zs, pl.ds(h * half, half), :]

    def forward_rest(h):
        for k in range(1, 4):
            a1[h][k - 1].wait_recv()
            forward(h, (z - k + 4) % 4)

    a3 = ([], [])

    def swap_start(h):
        for k in range(4):
            if k > 0:
                a2_copy(h, (i + k) % 4, k).wait_recv()
            piece = hblk.at[rows(h, (i - k + 4) % 4), mine]
            cp = remote(piece, piece, a3s.at[h, k], a3r.at[h, k], to_sib)
            cp.start()
            a3[h].append(cp)

    def swap_end(h):
        for cp in a3[h]:
            cp.wait_recv()

    def partial_logits(h):
        x = hblk[pl.ds(h * group, group), :]

        @pl.loop(0, voc // 256)
        def _(t):
            col = pl.ds(pl.multiple_of(t * 256, 256), 256)
            part[h, :, col] = jnp.dot(x, head_v[:, col], preferred_element_type=F32)

    lo, hi = pl.ds(0, quart), pl.ds(quart, quart)
    b = ([], [])

    def send_b(h, src, dst, to):
        n = len(b[h])
        cp = remote(src, dst, bs.at[h, n], br.at[h, n], to)
        cp.start()
        b[h].append(cp)

    def p_lo(h, block):
        return part.at[h, cut(block, 0, quart), :]

    def p_hi(h, block):
        return part.at[h, cut(block, quart, quart), :]

    def sum_start(h):
        send_b(h, p_lo(h, nd), relay.at[h, 0], to_x)
        send_b(h, p_hi(h, nd), relay.at[h, 1], to_y)
        send_b(h, p_lo(h, nx), got.at[h, 0, lo, :], to_x)
        send_b(h, p_hi(h, ny), got.at[h, 1, hi, :], to_y)

    def sum_relay(h):
        b[h][0].wait_recv()
        p_lo(h, ny)[...] = p_lo(h, ny)[...] + relay[h, 0]
        send_b(h, p_lo(h, ny), got.at[h, 1, lo, :], to_y)
        b[h][1].wait_recv()
        p_hi(h, nx)[...] = p_hi(h, nx)[...] + relay[h, 1]
        send_b(h, p_hi(h, nx), got.at[h, 0, hi, :], to_x)

    def teacher_rows(h):
        return tea_v[pl.ds(h * half, half), :].astype(F32)

    st = ([], [])

    def stats_start(h):
        for n in (2, 3, 4, 5):
            b[h][n].wait_recv()
        logits = part[h, cut(i), :] + got[h, 0] + got[h, 1]
        logits_v[h] = logits
        m = jnp.max(logits, axis=1, keepdims=True)
        e = jnp.exp(logits - m)
        s = jnp.sum(e, axis=1, keepdims=True)
        w = jnp.sum(e * (logits - teacher_rows(h)), axis=1, keepdims=True)
        lane = lax.broadcasted_iota(jnp.int32, (half, tok), 1)
        packed = jnp.where(lane == 0, m, jnp.where(lane == 1, s, w))
        packed = jnp.concatenate([packed, packed], axis=0)
        stat_v[h, j] = jnp.swapaxes(packed, 0, 1)[0:8, :]
        for k in range(1, 8):
            cp = remote(
                stat_v.at[h, j], stat_v.at[h, j], ss.at[h, k], sr.at[h, k],
                {"vocab": (j + k) % 8},
            )
            cp.start()
            st[h].append(cp)

    def gradient(h):
        for cp in st[h]:
            cp.wait_recv()
        stats = stat_v[h]
        tops = stats[:, 0, :]
        top = jnp.max(tops, axis=0, keepdims=True)
        scale = jnp.exp(tops - top)
        total = jnp.sum(stats[:, 1, :] * scale, axis=0, keepdims=True)
        weighted = jnp.sum(stats[:, 2, :] * scale, axis=0, keepdims=True)
        sub = lax.broadcasted_iota(jnp.int32, (tok, tok), 0)
        table = jnp.where(sub == 0, top, jnp.where(sub == 1, total, jnp.where(
            sub == 2, weighted / total, jnp.where(
                sub == 3, ids_v[...].astype(F32), mask_v[...].astype(F32)))))
        table = jnp.swapaxes(table, 0, 1)[h * half:(h + 1) * half, :]
        logits = logits_v[h]
        prob = jnp.exp(logits - table[:, 0:1]) / table[:, 1:2]
        gap = logits - teacher_rows(h)
        ids = table[:, 3:4].astype(jnp.int32) - j * voc
        onehot = (lax.broadcasted_iota(jnp.int32, (half, voc), 1) == ids).astype(F32)
        lg = table[:, 4:5] * (prob * (gap - table[:, 2:3]) + anchor_weight * (prob - onehot))
        lgb[rows(h, i), :] = lg.astype(BF16)

    cc = ([], [])

    def send_c(h, block, begin, to):
        n = len(cc[h])
        piece = lgb.at[rows(h, block, begin, quart), :]
        cp = remote(piece, piece, cs.at[h, n], cr.at[h, n], to)
        cp.start()
        cc[h].append(cp)

    def gather_start(h):
        send_c(h, i, 0, to_x)
        send_c(h, i, quart, to_y)
        send_c(h, i, quart, to_x)
        send_c(h, i, 0, to_y)
        cp = pltpu.make_async_copy(
            lgb.at[rows(h, i), :], lg_out.at[pl.ds(h * half, half), :], wsem.at[4 + h])
        cp.start()
        return cp

    def gather_relay(h):
        cc[h][0].wait_recv()
        send_c(h, nx, 0, to_y)
        cc[h][1].wait_recv()
        send_c(h, ny, quart, to_x)

    ecps = []

    def hidden_part(h):
        for n in (2, 3, 4, 5):
            cc[h][n].wait_recv()
        g = lgb[pl.ds(h * group, group), :]
        sib_out[h] = jnp.dot(g, head_t[:, other], preferred_element_type=F32).astype(BF16)
        cp = remote(sib_out.at[h], sib_in.at[h], es.at[h], er.at[h], to_sib)
        cp.start()
        ecps.append(cp)
        hown[h] = jnp.dot(g, head_t[:, mine], preferred_element_type=F32)

    def d2_copy(h, r, shift, zt):
        return remote(
            d1_in.at[h, r], d2_in.at[h, shift], d2s.at[h, shift], d2r.at[h, shift],
            {"vocab": zt * 2 + c},
        )

    def d2_send(h, r):
        zt = rel[r]
        shift = (zt - z + 4) % 4

        @pl.when(shift != 0)
        def _():
            d2_copy(h, r, shift, zt).start()

        @pl.when(shift == 0)
        def _():
            d2_in[h, 0] = d1_in[h, r]

    d1 = ([], [])

    def scatter_start(h):
        ecps[h].wait_recv()
        d1_out[h] = (hown[h] + sib_in[h].astype(F32)).astype(BF16)
        for r in (3, 1, 2):
            cp = remote(
                d1_out.at[h, cut(rel[r]), :], d1_in.at[h, r], d1s.at[h, r], d1r.at[h, r], to_rel[r])
            cp.start()
            d1[h].append(cp)
        d1_in[h, 0] = d1_out[h, cut(i), :]
        d2_send(h, 0)

    def scatter_relay(h):
        for n, r in ((1, 1), (2, 2), (0, 3)):
            d1[h][n].wait_recv()
            d2_send(h, r)

    def scatter_end(h):
        for k in range(1, 4):
            d2_copy(h, 0, k, (z + k) % 4).wait_recv()
        acc = d2_in[h, 0].astype(F32)
        for k in range(1, 4):
            acc = acc + d2_in[h, k].astype(F32)
        hg_v[pl.ds(h * half, half), :] = acc
        piece = pl.ds(h * half, half)
        cp = pltpu.make_async_copy(hg_v.at[piece, :], hg_out.at[piece, :], wsem.at[6 + h])
        cp.start()
        return cp

    wcps = []
    quarter = width // 4

    def weight_part(t):
        band = pl.ds(t * quarter, quarter)

        @pl.loop(0, voc // 256)
        def _(u):
            col = pl.ds(pl.multiple_of(u * 256, 256), 256)
            wg_v[band, col] = jnp.dot(
                hid_t[band, :], lgb[:, col], preferred_element_type=F32).astype(BF16)

        cp = pltpu.make_async_copy(wg_v.at[band, :], wg_out.at[band, :], wsem.at[t])
        cp.start()
        wcps.append(cp)

    def turn_head(t):
        band = pl.ds(t * quarter, quarter)
        head_t[:, band] = jnp.swapaxes(head_v[band, :], 0, 1)

    def turn_hidden(h):
        group_rows = pl.ds(h * group, group)

        @pl.loop(0, width // 256)
        def _(t):
            band = pl.ds(pl.multiple_of(t * 256, 256), 256)
            hid_t[band, group_rows] = jnp.swapaxes(hblk[group_rows, band], 0, 1)

    cp_hid.wait()
    send_a1(0)
    forward(0, z)
    for cp in a1[0]:
        cp.wait_send()
    send_a1(1)
    cp_head.wait()
    turn_head(0)
    forward_rest(0)
    turn_head(1)
    swap_start(0)
    turn_head(2)
    swap_end(0)
    partial_logits(0)
    sum_start(0)
    forward(1, z)
    forward_rest(1)
    cp_tea.wait()
    tea_v[own_trow, :] = tea_src[:, own_cols]
    tcps = []
    for k in range(1, 8):
        jt = (j + k) % 8
        cp = remote(
            tea_src.at[:, pl.ds(pl.multiple_of(jt * voc, voc), voc)], tea_v.at[own_trow, :],
            ts.at[k], tr.at[k], {"vocab": jt},
        )
        cp.start()
        tcps.append(cp)
    turn_head(3)
    sum_relay(0)
    swap_start(1)
    swap_end(1)
    partial_logits(1)
    sum_start(1)
    for cp in tcps:
        cp.wait_recv()
    cp_ids.wait()
    cp_mask.wait()
    stats_start(0)
    turn_hidden(0)
    gradient(0)
    sum_relay(1)
    out_cps = [gather_start(0)]
    turn_hidden(1)
    gather_relay(0)
    stats_start(1)
    gradient(1)
    out_cps.append(gather_start(1))
    hidden_part(0)
    gather_relay(1)
    scatter_start(0)
    hidden_part(1)
    scatter_relay(0)
    scatter_start(1)
    weight_part(0)
    weight_part(1)
    scatter_relay(1)
    weight_part(2)
    weight_part(3)
    out_cps.append(scatter_end(0))
    out_cps.append(scatter_end(1))

    for cp in a1[1] + tcps + ecps:
        cp.wait_send()
    for h in range(2):
        for cp in a3[h] + b[h] + st[h] + cc[h] + d1[h]:
            cp.wait_send()
        for k in range(1, 4):
            a2_copy(h, (i + k) % 4, k).wait_send()
            d2_copy(h, 0, k, (z + k) % 4).wait_send()
    for cp in wcps + out_cps:
        cp.wait()


def store(lg_ref, hg_ref, wg_ref, lg_out, hg_out, wg_out, lg_v, hg_v, wg_v, load_sem, store_sem):
    quarter = wg_ref.shape[0] // 4
    steps = [(wg_ref.at[pl.ds(t * quarter, quarter), :], wg_v.at[pl.ds(t * quarter, quarter), :],
              wg_out.at[pl.ds(t * quarter, quarter), :]) for t in range(4)]
    steps += [(lg_ref, lg_v, lg_out), (hg_ref, hg_v, hg_out)]
    loads = [pltpu.make_async_copy(a, v, load_sem.at[n]) for n, (a, v, o) in enumerate(steps)]
    stores = [pltpu.make_async_copy(v, o, store_sem.at[n]) for n, (a, v, o) in enumerate(steps)]
    for cp in loads:
        cp.start()
    for load, save in zip(loads, stores):
        load.wait()
        save.start()
    for cp in stores:
        cp.wait()


def fused(hidden_states, teacher_logprob, head_weight, token_ids, padding_mask):
    tok, feat = hidden_states.shape
    width, voc = head_weight.shape
    trow = teacher_logprob.shape[0]
    half = tok // 2
    any_spec = pl.BlockSpec(memory_space=pl.ANY)
    dma = pltpu.SemaphoreType.DMA
    held = pl.pallas_call(
        kernel,
        out_shape=(
            jax.ShapeDtypeStruct((tok, voc), BF16),
            jax.ShapeDtypeStruct((tok, feat), F32),
            jax.ShapeDtypeStruct((width, voc), BF16),
        ),
        in_specs=[pl.BlockSpec(memory_space=pltpu.HBM)] * 5,
        out_specs=[any_spec] * 3,
        scratch_shapes=[
            pltpu.VMEM((width, voc), BF16),
            pltpu.VMEM((voc, width), BF16),
            pltpu.VMEM((4, tok, feat), BF16),
            pltpu.VMEM((4 * tok, width), BF16),
            pltpu.VMEM((width, 4 * tok), BF16),
            pltpu.VMEM(teacher_logprob.shape, BF16),
            pltpu.VMEM((8 * trow, voc), BF16),
            pltpu.VMEM((1, tok), jnp.int32),
            pltpu.VMEM((1, tok), jnp.int32),
            pltpu.VMEM((2, 4 * half, voc), F32),
            pltpu.VMEM((2, 2, half // 2, voc), F32),
            pltpu.VMEM((2, 2, half, voc), F32),
            pltpu.VMEM((2, half, voc), F32),
            pltpu.VMEM((2, 8, 8, tok), F32),
            pltpu.VMEM((4 * tok, voc), BF16),
            pltpu.VMEM((2, 4 * half, feat), F32),
            pltpu.VMEM((2, 4 * half, feat), BF16),
            pltpu.VMEM((2, 4 * half, feat), BF16),
            pltpu.VMEM((2, 4 * half, feat), BF16),
            pltpu.VMEM((2, 4, half, feat), BF16),
            pltpu.VMEM((2, 4, half, feat), BF16),
            pltpu.VMEM((width, voc), BF16),
            pltpu.VMEM((tok, feat), F32),
            dma((5,)), dma((2, 4)), dma((2, 4)), dma((2, 4)), dma((2, 4)), dma((2, 4)), dma((2, 4)),
            dma((8,)), dma((8,)), dma((2, 6)), dma((2, 6)), dma((2, 8)), dma((2, 8)),
            dma((2, 6)), dma((2, 6)), dma((2,)), dma((2,)), dma((2, 4)), dma((2, 4)),
            dma((2, 4)), dma((2, 4)), dma((8,)),
        ],
        compiler_params=pltpu.CompilerParams(
            collective_id=0, has_side_effects=True, vmem_limit_bytes=62 * 1024 * 1024
        ),
        cost_estimate=pl.CostEstimate(
            flops=6 * 4 * tok * width * voc, bytes_accessed=6 * width * voc,
            transcendentals=2 * tok * voc,
        ),
    )(
        hidden_states, teacher_logprob, head_weight,
        token_ids.reshape(1, tok), padding_mask.reshape(1, tok),
    )
    return pl.pallas_call(
        store,
        out_shape=tuple(jax.ShapeDtypeStruct(x.shape, x.dtype) for x in held),
        in_specs=[any_spec] * 3,
        out_specs=[pl.BlockSpec(memory_space=pltpu.HBM)] * 3,
        scratch_shapes=[pltpu.VMEM(x.shape, x.dtype) for x in held] + [dma((6,)), dma((6,))],
        compiler_params=pltpu.CompilerParams(vmem_limit_bytes=62 * 1024 * 1024),
    )(*held)


def gathered(n_dp, n_vocab, hidden_states, teacher_logprob, head_weight, token_ids, padding_mask):
    voc = head_weight.shape[1]
    full = lax.all_gather(hidden_states, "vocab", axis=1, tiled=True)
    block = lax.all_to_all(full, "dp", split_axis=1, concat_axis=0, tiled=True)
    teacher = lax.all_to_all(teacher_logprob, "vocab", split_axis=1, concat_axis=0, tiled=True)
    part = jnp.dot(block, head_weight, preferred_element_type=F32)
    logits = lax.psum_scatter(part, "dp", scatter_dimension=0, tiled=True)
    gap = logits - teacher.astype(F32)
    top = lax.pmax(jnp.max(logits, axis=1), "vocab")
    expo = jnp.exp(logits - top[:, None])
    total, weighted = lax.psum((jnp.sum(expo, axis=1), jnp.sum(expo * gap, axis=1)), "vocab")
    columns = lax.axis_index("vocab") * voc + jnp.arange(voc, dtype=jnp.int32)
    onehot = (columns[None, :] == token_ids[:, None]).astype(F32)
    prob = expo / total[:, None]
    keep = padding_mask.astype(F32)[:, None]
    logit_grad = (
        keep * (prob * (gap - (weighted / total)[:, None]) + anchor_weight * (prob - onehot))
    ).astype(BF16)
    every = lax.all_gather(logit_grad, "dp", axis=0, tiled=True)
    head_grad = lax.dot_general(
        block, every, (((0,), (0,)), ((), ())), preferred_element_type=F32).astype(BF16)
    back = lax.dot_general(
        every, head_weight, (((1,), (1,)), ((), ())), preferred_element_type=F32)
    back = lax.all_to_all(back, "dp", split_axis=0, concat_axis=1, tiled=True)
    hidden_grad = lax.psum_scatter(back, "vocab", scatter_dimension=1, tiled=True)
    return (logit_grad, hidden_grad, head_grad)


def solution(mesh):
    in_specs = (P("dp", "vocab"), P(("dp", "vocab"), None), P("dp", "vocab"), P("dp"), P("dp"))
    out_specs = (P("dp", "vocab"), P("dp", "vocab"), P("dp", "vocab"))
    n_dp, n_vocab = mesh.shape["dp"], mesh.shape["vocab"]
    body = fused if (n_dp, n_vocab) == (4, 8) else functools.partial(gathered, n_dp, n_vocab)
    return jax.shard_map(body, mesh=mesh, in_specs=in_specs, out_specs=out_specs, check_vma=False)
```

```python
import functools
import jax
import jax.numpy as jnp
from jax import lax
from jax.experimental import pallas as pl
from jax.experimental.pallas import tpu as pltpu
from jax.sharding import PartitionSpec as P

anchor_weight = 0.25
MESH = pl.DeviceIdType.MESH
F32 = jnp.float32
BF16 = jnp.bfloat16


def kernel(
    hid_ref, tea_ref, head_ref, ids_ref, mask_ref,
    lg_out, hg_out, wg_out,
    head_v, head_t, zbuf, hblk, hid_t, tea_src, tea_v, ids_v, mask_v, part, relay, got, logits_v, stat_v,
    lgb, hown, sib_out, sib_in, d1_out, d1_in, d2_in, wg_v, hg_v,
    loc_sem, a1s, a1r, a2s, a2r, a3s, a3r, ts, tr, bs, br, ss, sr, cs, cr,
    es, er, d1s, d1r, d2s, d2r, wsem,
):
    tok, feat = hid_ref.shape
    width, voc = head_ref.shape
    half = tok // 4
    quart = half // 2
    group = 4 * half
    trow = tea_ref.shape[0]
    i, j = lax.axis_index("dp"), lax.axis_index("vocab")
    z, c = j // 2, j % 2
    sib = z * 2 + (1 - c)
    nx = i + 1 - 2 * (i % 2)
    ny = (i + 2) % 4
    nd = 3 - i
    rel = (i, nx, ny, nd)
    to_x, to_y, to_d = {"dp": nx}, {"dp": ny}, {"dp": nd}
    to_rel = (None, to_x, to_y, to_d)
    to_sib = {"vocab": sib}

    def remote(src, dst, ssem, rsem, to):
        return pltpu.make_async_remote_copy(
            src_ref=src, dst_ref=dst, send_sem=ssem, recv_sem=rsem,
            device_id=to, device_id_type=MESH,
        )

    def cut(block, begin=0, size=None):
        size = half if size is None else size
        return pl.ds(pl.multiple_of(block * half + begin, 16), size)

    def rows(h, block, begin=0, size=None):
        return cut(h * 4 + block, begin, size)

    mine = pl.ds(pl.multiple_of(c * feat, feat), feat)
    other = pl.ds(pl.multiple_of((1 - c) * feat, feat), feat)

    own_cols = pl.ds(pl.multiple_of(j * voc, voc), voc)
    own_trow = pl.ds(pl.multiple_of(j * trow, trow), trow)
    cp_hid = pltpu.make_async_copy(hid_ref, zbuf.at[z], loc_sem.at[0])
    cp_head = pltpu.make_async_copy(head_ref, head_v, loc_sem.at[1])
    cp_tea = pltpu.make_async_copy(tea_ref, tea_src, loc_sem.at[2])
    cp_ids = pltpu.make_async_copy(ids_ref, ids_v, loc_sem.at[3])
    cp_mask = pltpu.make_async_copy(mask_ref, mask_v, loc_sem.at[4])
    for cp in (cp_hid, cp_head, cp_tea, cp_ids, cp_mask):
        cp.start()

    barrier = pltpu.get_barrier_semaphore()
    for k in range(1, 4):
        pl.semaphore_signal(barrier, inc=1, device_id={"dp": (i + k) % 4}, device_id_type=MESH)
    for k in range(1, 8):
        pl.semaphore_signal(barrier, inc=1, device_id={"vocab": (j + k) % 8}, device_id_type=MESH)
    pl.semaphore_wait(barrier, 10)

    a1 = ([], [], [], [])

    def send_a1(h):
        piece = pl.ds(h * half, half)
        for k in range(1, 4):
            cp = remote(
                zbuf.at[z, piece, :], zbuf.at[z, piece, :], a1s.at[h, k], a1r.at[h, k],
                {"vocab": ((z + k) % 4) * 2 + c},
            )
            cp.start()
            a1[h].append(cp)

    def a2_copy(h, zs, shift):
        return remote(
            zbuf.at[zs, pl.ds(h * half, half), :], hblk.at[rows(h, i), mine],
            a2s.at[h, shift], a2r.at[h, shift], {"dp": zs},
        )

    def forward(h, zs):
        shift = (zs - i + 4) % 4

        @pl.when(shift != 0)
        def _():
            a2_copy(h, zs, shift).start()

        @pl.when(shift == 0)
        def _():
            hblk[rows(h, i), mine] = zbuf[zs, pl.ds(h * half, half), :]

    def forward_rest(h):
        for k in range(1, 4):
            a1[h][k - 1].wait_recv()
            forward(h, (z - k + 4) % 4)

    a3 = ([], [], [], [])

    def swap_start(h):
        for k in range(4):
            if k > 0:
                a2_copy(h, (i + k) % 4, k).wait_recv()
            piece = hblk.at[rows(h, (i - k + 4) % 4), mine]
            cp = remote(piece, piece, a3s.at[h, k], a3r.at[h, k], to_sib)
            cp.start()
            a3[h].append(cp)

    def swap_end(h):
        for cp in a3[h]:
            cp.wait_recv()

    def partial_logits(h):
        x = hblk[pl.ds(h * group, group), :]

        @pl.loop(0, voc // 256)
        def _(t):
            col = pl.ds(pl.multiple_of(t * 256, 256), 256)
            part[h, :, col] = jnp.dot(x, head_v[:, col], preferred_element_type=F32)

    lo, hi = pl.ds(0, quart), pl.ds(quart, quart)
    b = ([], [], [], [])

    def send_b(h, src, dst, to):
        n = len(b[h])
        cp = remote(src, dst, bs.at[h, n], br.at[h, n], to)
        cp.start()
        b[h].append(cp)

    def p_lo(h, block):
        return part.at[h, cut(block, 0, quart), :]

    def p_hi(h, block):
        return part.at[h, cut(block, quart, quart), :]

    def sum_start(h):
        send_b(h, p_lo(h, nd), relay.at[h, 0], to_x)
        send_b(h, p_hi(h, nd), relay.at[h, 1], to_y)
        send_b(h, p_lo(h, nx), got.at[h, 0, lo, :], to_x)
        send_b(h, p_hi(h, ny), got.at[h, 1, hi, :], to_y)

    def sum_relay(h):
        b[h][0].wait_recv()
        p_lo(h, ny)[...] = p_lo(h, ny)[...] + relay[h, 0]
        send_b(h, p_lo(h, ny), got.at[h, 1, lo, :], to_y)
        b[h][1].wait_recv()
        p_hi(h, nx)[...] = p_hi(h, nx)[...] + relay[h, 1]
        send_b(h, p_hi(h, nx), got.at[h, 0, hi, :], to_x)

    def teacher_rows(h):
        return tea_v[pl.ds(h * half, half), :].astype(F32)

    st = ([], [], [], [])

    def stats_start(h):
        for n in (2, 3, 4, 5):
            b[h][n].wait_recv()
        logits = part[h, cut(i), :] + got[h, 0] + got[h, 1]
        logits_v[h] = logits
        m = jnp.max(logits, axis=1, keepdims=True)
        e = jnp.exp(logits - m)
        s = jnp.sum(e, axis=1, keepdims=True)
        w = jnp.sum(e * (logits - teacher_rows(h)), axis=1, keepdims=True)
        lane = lax.broadcasted_iota(jnp.int32, (half, tok), 1)
        packed = jnp.where(lane == 0, m, jnp.where(lane == 1, s, w))
        packed = jnp.concatenate([packed] * 4, axis=0)
        stat_v[h, j] = jnp.swapaxes(packed, 0, 1)[0:8, :]
        for k in range(1, 8):
            cp = remote(
                stat_v.at[h, j], stat_v.at[h, j], ss.at[h, k], sr.at[h, k],
                {"vocab": (j + k) % 8},
            )
            cp.start()
            st[h].append(cp)

    def gradient(h):
        for cp in st[h]:
            cp.wait_recv()
        stats = stat_v[h]
        tops = stats[:, 0, :]
        top = jnp.max(tops, axis=0, keepdims=True)
        scale = jnp.exp(tops - top)
        total = jnp.sum(stats[:, 1, :] * scale, axis=0, keepdims=True)
        weighted = jnp.sum(stats[:, 2, :] * scale, axis=0, keepdims=True)
        sub = lax.broadcasted_iota(jnp.int32, (tok, tok), 0)
        table = jnp.where(sub == 0, top, jnp.where(sub == 1, total, jnp.where(
            sub == 2, weighted / total, jnp.where(
                sub == 3, ids_v[...].astype(F32), mask_v[...].astype(F32)))))
        table = jnp.swapaxes(table, 0, 1)[h * half:(h + 1) * half, :]
        logits = logits_v[h]
        prob = jnp.exp(logits - table[:, 0:1]) / table[:, 1:2]
        gap = logits - teacher_rows(h)
        ids = table[:, 3:4].astype(jnp.int32) - j * voc
        onehot = (lax.broadcasted_iota(jnp.int32, (half, voc), 1) == ids).astype(F32)
        lg = table[:, 4:5] * (prob * (gap - table[:, 2:3]) + anchor_weight * (prob - onehot))
        lgb[rows(h, i), :] = lg.astype(BF16)

    cc = ([], [], [], [])

    def send_c(h, block, begin, to):
        n = len(cc[h])
        piece = lgb.at[rows(h, block, begin, quart), :]
        cp = remote(piece, piece, cs.at[h, n], cr.at[h, n], to)
        cp.start()
        cc[h].append(cp)

    def gather_start(h):
        send_c(h, i, 0, to_x)
        send_c(h, i, quart, to_y)
        send_c(h, i, quart, to_x)
        send_c(h, i, 0, to_y)
        cp = pltpu.make_async_copy(
            lgb.at[rows(h, i), :], lg_out.at[pl.ds(h * half, half), :], wsem.at[4 + h])
        cp.start()
        return cp

    def gather_relay(h):
        cc[h][0].wait_recv()
        send_c(h, nx, 0, to_y)
        cc[h][1].wait_recv()
        send_c(h, ny, quart, to_x)

    ecps = []

    def hidden_part(h):
        for n in (2, 3, 4, 5):
            cc[h][n].wait_recv()
        g = lgb[pl.ds(h * group, group), :]
        sib_out[h] = jnp.dot(g, head_t[:, other], preferred_element_type=F32).astype(BF16)
        cp = remote(sib_out.at[h], sib_in.at[h], es.at[h], er.at[h], to_sib)
        cp.start()
        ecps.append(cp)
        hown[h] = jnp.dot(g, head_t[:, mine], preferred_element_type=F32)

    def d2_copy(h, r, shift, zt):
        return remote(
            d1_in.at[h, r], d2_in.at[h, shift], d2s.at[h, shift], d2r.at[h, shift],
            {"vocab": zt * 2 + c},
        )

    def d2_send(h, r):
        zt = rel[r]
        shift = (zt - z + 4) % 4

        @pl.when(shift != 0)
        def _():
            d2_copy(h, r, shift, zt).start()

        @pl.when(shift == 0)
        def _():
            d2_in[h, 0] = d1_in[h, r]

    d1 = ([], [], [], [])

    def scatter_start(h):
        ecps[h].wait_recv()
        d1_out[h] = (hown[h] + sib_in[h].astype(F32)).astype(BF16)
        for r in (3, 1, 2):
            cp = remote(
                d1_out.at[h, cut(rel[r]), :], d1_in.at[h, r], d1s.at[h, r], d1r.at[h, r], to_rel[r])
            cp.start()
            d1[h].append(cp)
        d1_in[h, 0] = d1_out[h, cut(i), :]
        d2_send(h, 0)

    def scatter_relay(h):
        for n, r in ((1, 1), (2, 2), (0, 3)):
            d1[h][n].wait_recv()
            d2_send(h, r)

    def scatter_end(h):
        for k in range(1, 4):
            d2_copy(h, 0, k, (z + k) % 4).wait_recv()
        acc = d2_in[h, 0].astype(F32)
        for k in range(1, 4):
            acc = acc + d2_in[h, k].astype(F32)
        hg_v[pl.ds(h * half, half), :] = acc
        piece = pl.ds(h * half, half)
        cp = pltpu.make_async_copy(hg_v.at[piece, :], hg_out.at[piece, :], wsem.at[8 + h])
        cp.start()
        return cp

    wcps = []
    quarter = width // 4

    def weight_part(t):
        band = pl.ds(t * quarter, quarter)

        @pl.loop(0, voc // 256)
        def _(u):
            col = pl.ds(pl.multiple_of(u * 256, 256), 256)
            wg_v[band, col] = jnp.dot(
                hid_t[band, :], lgb[:, col], preferred_element_type=F32).astype(BF16)

        cp = pltpu.make_async_copy(wg_v.at[band, :], wg_out.at[band, :], wsem.at[t])
        cp.start()
        wcps.append(cp)

    def turn_head(t):
        band = pl.ds(t * quarter, quarter)
        head_t[:, band] = jnp.swapaxes(head_v[band, :], 0, 1)

    def turn_hidden(h):
        group_rows = pl.ds(h * group, group)

        @pl.loop(0, width // 256)
        def _(t):
            band = pl.ds(pl.multiple_of(t * 256, 256), 256)
            hid_t[band, group_rows] = jnp.swapaxes(hblk[group_rows, band], 0, 1)

    def logits_start(h):
        swap_start(h)
        swap_end(h)
        partial_logits(h)
        sum_start(h)

    out_cps = []

    cp_hid.wait()
    send_a1(0)
    forward(0, z)
    for cp in a1[0]:
        cp.wait_send()
    send_a1(1)
    cp_head.wait()
    turn_head(0)
    forward_rest(0)
    turn_head(1)
    swap_start(0)
    turn_head(2)
    swap_end(0)
    partial_logits(0)
    sum_start(0)
    send_a1(2)
    forward(1, z)
    forward_rest(1)
    send_a1(3)
    cp_tea.wait()
    tea_v[own_trow, :] = tea_src[:, own_cols]
    tcps = []
    for k in range(1, 8):
        jt = (j + k) % 8
        cp = remote(
            tea_src.at[:, pl.ds(pl.multiple_of(jt * voc, voc), voc)], tea_v.at[own_trow, :],
            ts.at[k], tr.at[k], {"vocab": jt},
        )
        cp.start()
        tcps.append(cp)
    turn_head(3)
    sum_relay(0)
    logits_start(1)
    forward(2, z)
    forward_rest(2)
    for cp in tcps:
        cp.wait_recv()
    cp_ids.wait()
    cp_mask.wait()
    stats_start(0)
    turn_hidden(0)
    sum_relay(1)
    gradient(0)
    out_cps.append(gather_start(0))
    logits_start(2)
    forward(3, z)
    forward_rest(3)
    stats_start(1)
    turn_hidden(1)
    gather_relay(0)
    sum_relay(2)
    gradient(1)
    out_cps.append(gather_start(1))
    logits_start(3)
    hidden_part(0)
    stats_start(2)
    turn_hidden(2)
    gather_relay(1)
    scatter_start(0)
    sum_relay(3)
    gradient(2)
    out_cps.append(gather_start(2))
    hidden_part(1)
    stats_start(3)
    turn_hidden(3)
    gather_relay(2)
    scatter_start(1)
    scatter_relay(0)
    gradient(3)
    out_cps.append(gather_start(3))
    hidden_part(2)
    gather_relay(3)
    scatter_start(2)
    scatter_relay(1)
    hidden_part(3)
    scatter_relay(2)
    scatter_start(3)
    weight_part(0)
    weight_part(1)
    scatter_relay(3)
    weight_part(2)
    weight_part(3)
    for h in range(4):
        out_cps.append(scatter_end(h))

    for cp in a1[1] + a1[2] + a1[3] + tcps + ecps:
        cp.wait_send()
    for h in range(4):
        for cp in a3[h] + b[h] + st[h] + cc[h] + d1[h]:
            cp.wait_send()
        for k in range(1, 4):
            a2_copy(h, (i + k) % 4, k).wait_send()
            d2_copy(h, 0, k, (z + k) % 4).wait_send()
    for cp in wcps + out_cps:
        cp.wait()


def store(lg_ref, hg_ref, wg_ref, lg_out, hg_out, wg_out, lg_v, hg_v, wg_v, load_sem, store_sem):
    quarter = wg_ref.shape[0] // 4
    steps = [(wg_ref.at[pl.ds(t * quarter, quarter), :], wg_v.at[pl.ds(t * quarter, quarter), :],
              wg_out.at[pl.ds(t * quarter, quarter), :]) for t in range(4)]
    steps += [(lg_ref, lg_v, lg_out), (hg_ref, hg_v, hg_out)]
    loads = [pltpu.make_async_copy(a, v, load_sem.at[n]) for n, (a, v, o) in enumerate(steps)]
    stores = [pltpu.make_async_copy(v, o, store_sem.at[n]) for n, (a, v, o) in enumerate(steps)]
    for cp in loads:
        cp.start()
    for load, save in zip(loads, stores):
        load.wait()
        save.start()
    for cp in stores:
        cp.wait()


def fused(hidden_states, teacher_logprob, head_weight, token_ids, padding_mask):
    tok, feat = hidden_states.shape
    width, voc = head_weight.shape
    trow = teacher_logprob.shape[0]
    half = tok // 4
    any_spec = pl.BlockSpec(memory_space=pl.ANY)
    dma = pltpu.SemaphoreType.DMA
    held = pl.pallas_call(
        kernel,
        out_shape=(
            jax.ShapeDtypeStruct((tok, voc), BF16),
            jax.ShapeDtypeStruct((tok, feat), F32),
            jax.ShapeDtypeStruct((width, voc), BF16),
        ),
        in_specs=[pl.BlockSpec(memory_space=pltpu.HBM)] * 5,
        out_specs=[any_spec] * 3,
        scratch_shapes=[
            pltpu.VMEM((width, voc), BF16),
            pltpu.VMEM((voc, width), BF16),
            pltpu.VMEM((4, tok, feat), BF16),
            pltpu.VMEM((4 * tok, width), BF16),
            pltpu.VMEM((width, 4 * tok), BF16),
            pltpu.VMEM(teacher_logprob.shape, BF16),
            pltpu.VMEM((8 * trow, voc), BF16),
            pltpu.VMEM((1, tok), jnp.int32),
            pltpu.VMEM((1, tok), jnp.int32),
            pltpu.VMEM((4, 4 * half, voc), F32),
            pltpu.VMEM((4, 2, half // 2, voc), F32),
            pltpu.VMEM((4, 2, half, voc), F32),
            pltpu.VMEM((4, half, voc), F32),
            pltpu.VMEM((4, 8, 8, tok), F32),
            pltpu.VMEM((4 * tok, voc), BF16),
            pltpu.VMEM((4, 4 * half, feat), F32),
            pltpu.VMEM((4, 4 * half, feat), BF16),
            pltpu.VMEM((4, 4 * half, feat), BF16),
            pltpu.VMEM((4, 4 * half, feat), BF16),
            pltpu.VMEM((4, 4, half, feat), BF16),
            pltpu.VMEM((4, 4, half, feat), BF16),
            pltpu.VMEM((width, voc), BF16),
            pltpu.VMEM((tok, feat), F32),
            dma((5,)), dma((4, 4)), dma((4, 4)), dma((4, 4)), dma((4, 4)), dma((4, 4)), dma((4, 4)),
            dma((8,)), dma((8,)), dma((4, 6)), dma((4, 6)), dma((4, 8)), dma((4, 8)),
            dma((4, 6)), dma((4, 6)), dma((4,)), dma((4,)), dma((4, 4)), dma((4, 4)),
            dma((4, 4)), dma((4, 4)), dma((12,)),
        ],
        compiler_params=pltpu.CompilerParams(
            collective_id=0, has_side_effects=True, vmem_limit_bytes=62 * 1024 * 1024
        ),
        cost_estimate=pl.CostEstimate(
            flops=6 * 4 * tok * width * voc, bytes_accessed=6 * width * voc,
            transcendentals=2 * tok * voc,
        ),
    )(
        hidden_states, teacher_logprob, head_weight,
        token_ids.reshape(1, tok), padding_mask.reshape(1, tok),
    )
    return pl.pallas_call(
        store,
        out_shape=tuple(jax.ShapeDtypeStruct(x.shape, x.dtype) for x in held),
        in_specs=[any_spec] * 3,
        out_specs=[pl.BlockSpec(memory_space=pltpu.HBM)] * 3,
        scratch_shapes=[pltpu.VMEM(x.shape, x.dtype) for x in held] + [dma((6,)), dma((6,))],
        compiler_params=pltpu.CompilerParams(vmem_limit_bytes=62 * 1024 * 1024),
    )(*held)


def gathered(n_dp, n_vocab, hidden_states, teacher_logprob, head_weight, token_ids, padding_mask):
    voc = head_weight.shape[1]
    full = lax.all_gather(hidden_states, "vocab", axis=1, tiled=True)
    block = lax.all_to_all(full, "dp", split_axis=1, concat_axis=0, tiled=True)
    teacher = lax.all_to_all(teacher_logprob, "vocab", split_axis=1, concat_axis=0, tiled=True)
    part = jnp.dot(block, head_weight, preferred_element_type=F32)
    logits = lax.psum_scatter(part, "dp", scatter_dimension=0, tiled=True)
    gap = logits - teacher.astype(F32)
    top = lax.pmax(jnp.max(logits, axis=1), "vocab")
    expo = jnp.exp(logits - top[:, None])
    total, weighted = lax.psum((jnp.sum(expo, axis=1), jnp.sum(expo * gap, axis=1)), "vocab")
    columns = lax.axis_index("vocab") * voc + jnp.arange(voc, dtype=jnp.int32)
    onehot = (columns[None, :] == token_ids[:, None]).astype(F32)
    prob = expo / total[:, None]
    keep = padding_mask.astype(F32)[:, None]
    logit_grad = (
        keep * (prob * (gap - (weighted / total)[:, None]) + anchor_weight * (prob - onehot))
    ).astype(BF16)
    every = lax.all_gather(logit_grad, "dp", axis=0, tiled=True)
    head_grad = lax.dot_general(
        block, every, (((0,), (0,)), ((), ())), preferred_element_type=F32).astype(BF16)
    back = lax.dot_general(
        every, head_weight, (((1,), (1,)), ((), ())), preferred_element_type=F32)
    back = lax.all_to_all(back, "dp", split_axis=0, concat_axis=1, tiled=True)
    hidden_grad = lax.psum_scatter(back, "vocab", scatter_dimension=1, tiled=True)
    return (logit_grad, hidden_grad, head_grad)


def solution(mesh):
    in_specs = (P("dp", "vocab"), P(("dp", "vocab"), None), P("dp", "vocab"), P("dp"), P("dp"))
    out_specs = (P("dp", "vocab"), P("dp", "vocab"), P("dp", "vocab"))
    n_dp, n_vocab = mesh.shape["dp"], mesh.shape["vocab"]
    body = fused if (n_dp, n_vocab) == (4, 8) else functools.partial(gathered, n_dp, n_vocab)
    return jax.shard_map(body, mesh=mesh, in_specs=in_specs, out_specs=out_specs, check_vma=False)
```
